128 devices in a mesh: row: 16 (over x, y_hi, core), col: 8 (over y_lo, z).
Axes of the slice: x: 4, y: 4 (y_hi: 2, y_lo: 2; y = y_hi * 2 + y_lo), z: 4, core: 2. Of those that a mesh axis runs over, the one named last changes fastest.
Arguments:
- final_amp: bfloat16 [16, 32, 128, 440], P('row', 'col'), may hold values from -0.19921875 to 0.19921875
- initial_amp: bfloat16 [8, 32, 128, 440], P('col', 'row'), may hold values from -0.19921875 to 0.19921875
- pair_final: int32 [16, 8, 128], P('row', 'col'), may hold values from 0 to 31
- pair_initial: int32 [16, 8, 128], P('row', 'col'), may hold values from 0 to 31
- map_final: int32 [16, 32, 440], P('row', 'col'), may hold values from 0 to 439, each once within a row
- map_initial: int32 [8, 32, 440], P('col', 'row'), may hold values from 0 to 439, each once within a row
- counts: int32 [16, 8], P('row', 'col'), may hold values from 16 to 128, as said below
Outputs:
- density: float32 [440, 440], replicated
The draws below stay inside these ranges and needn't reach their ends.
Inputs may be any that keep to these rules, and one draw needn't show every extreme that they name: `counts`: slots at or past a cell's count are ignored. Exactly one cell of every draw has 128 live slots.
All inputs are finite; a program needn't handle non-finite values.
Results may differ from the reference program's by a relative error of at most 0.0003.
Values may be sent and summed in bfloat16 or wider, within the bound.
No kernel may reach another device: no remote copies, remote signals or barrier semaphores. Data moves between devices by JAX's collectives and lax.ppermute only.
A program may use at most 64 MiB of HBM per device.

```python
import jax
import jax.numpy as jnp
from jax import lax

ORB = 440
BLK = 128
SEGB = 32
K = 128
GROUP = 32
GRID_ROWS = 16
GRID_COLS = 8


def draw_counts(key, part):
    base_key, busy_key = jax.random.split(jax.random.fold_in(key, 11))
    base = jax.random.randint(base_key, (GRID_ROWS, GRID_COLS), K // 8, K // 2 + 1, dtype=jnp.int32)
    busiest = jax.random.randint(busy_key, (), 0, GRID_ROWS * GRID_COLS, dtype=jnp.int32)
    cells = jnp.arange(GRID_ROWS * GRID_COLS, dtype=jnp.int32).reshape(GRID_ROWS, GRID_COLS)
    return jnp.where(cells == busiest, K, base).astype(jnp.int32)


def plant(entries, key, smallest, top_value):
    place = [jax.random.randint(jax.random.fold_in(key, axis), (), 0, length) for axis, length in enumerate(entries.shape)]
    widest = entries.shape.index(max(entries.shape))
    next_to = place[:widest] + [(place[widest] + 1) % entries.shape[widest]] + place[widest + 1:]
    return entries.at[tuple(place)].set(smallest).at[tuple(next_to)].set(top_value)


def shard_levels(rng, extent, pieces, smallest, top_value):
    def one(dim, blocks):
        steps = jax.random.uniform(jax.random.fold_in(jax.random.fold_in(rng, 6), dim), (blocks,), jnp.float32, smallest / len(pieces), top_value / len(pieces))
        return jnp.repeat(jnp.exp(steps), extent[dim] // blocks).reshape((-1,) + (1,) * (len(extent) - dim - 1))

    loudness = one(*pieces[0])
    for cut in pieces[1:]:
        loudness = loudness * one(*cut)
    return loudness


def centred(rng, dims, scale, reach, cuts=(), kind=jnp.bfloat16):
    level = shard_levels(rng, dims, cuts, -0.22, 0.18) if cuts else 1.0
    array = jax.random.normal(rng, dims, jnp.float32) * scale * level
    return jnp.minimum(jnp.maximum(array, -reach), reach).astype(kind)


def setup_inputs(seed: int = 0) -> dict:
    splits = jax.random.split(jax.random.key(seed), 8)
    return {
        "final_amp": centred(splits[0], (GRID_ROWS, SEGB, BLK, ORB), 0.03, 0.19921875, ((0, 16), (1, 8))),
        "initial_amp": centred(splits[1], (GRID_COLS, SEGB, BLK, ORB), 0.03, 0.19921875, ((0, 8), (1, 16))),
        "pair_final": plant(jax.random.randint(splits[2], (GRID_ROWS, GRID_COLS, K), 0, SEGB), jax.random.fold_in(splits[2], 1), 0, SEGB - 1).astype(jnp.int32),
        "pair_initial": plant(jax.random.randint(splits[3], (GRID_ROWS, GRID_COLS, K), 0, SEGB), jax.random.fold_in(splits[3], 1), 0, SEGB - 1).astype(jnp.int32),
        "map_final": jax.vmap(lambda own: jax.random.permutation(own, ORB))(jax.random.split(splits[4], GRID_ROWS * SEGB)).reshape((GRID_ROWS, SEGB, ORB)).astype(jnp.int32),
        "map_initial": jax.vmap(lambda own: jax.random.permutation(own, ORB))(jax.random.split(splits[5], GRID_COLS * SEGB)).reshape((GRID_COLS, SEGB, ORB)).astype(jnp.int32),
        "counts": draw_counts(jax.random.fold_in(splits[7], 71), 0),
    }


def permute_columns(blocks, orbital_map):
    return jnp.take(blocks, orbital_map, axis=1)


def cell_density(final_seg, initial_seg, slots_final, slots_initial, live_count):
    def advance(index, summed):
        first_slot = index * GROUP
        which_final = lax.dynamic_slice_in_dim(slots_final, first_slot, GROUP)
        which_initial = lax.dynamic_slice_in_dim(slots_initial, first_slot, GROUP)
        live_mask = (first_slot + jnp.arange(GROUP, dtype=jnp.int32)) < live_count
        left = jnp.take(final_seg, which_final, axis=0)
        right = jnp.take(initial_seg, which_initial, axis=0)
        left = jnp.where(live_mask[:, None, None], left, jnp.zeros_like(left))
        return summed + jnp.dot(left.reshape(-1, ORB).T, right.reshape(-1, ORB), preferred_element_type=jnp.float32)

    turns = (live_count + GROUP - 1) // GROUP
    return lax.fori_loop(0, turns, advance, jnp.zeros((ORB, ORB), jnp.float32))


def reference(final_amp, initial_amp, pair_final, pair_initial, map_final, map_initial, counts):
    def add_cell(cell, summed):
        brow = cell // GRID_COLS
        bcol = cell % GRID_COLS
        final_seg = lax.dynamic_index_in_dim(final_amp, brow, 0, keepdims=False)
        initial_seg = lax.dynamic_index_in_dim(initial_amp, bcol, 0, keepdims=False)
        fmap = lax.dynamic_index_in_dim(map_final, brow, 0, keepdims=False)
        imap = lax.dynamic_index_in_dim(map_initial, bcol, 0, keepdims=False)
        final_seg = jax.vmap(permute_columns)(final_seg, fmap)
        initial_seg = jax.vmap(permute_columns)(initial_seg, imap)
        return summed + cell_density(final_seg, initial_seg, pair_final[brow, bcol], pair_initial[brow, bcol], counts[brow, bcol])

    return lax.fori_loop(0, GRID_ROWS * GRID_COLS, add_cell, jnp.zeros((ORB, ORB), jnp.float32))
```

```python
import jax
import jax.numpy as jnp
from jax import lax
from jax.experimental import pallas as pl
from jax.experimental.pallas import tpu as pltpu
from jax.sharding import PartitionSpec as P

LANES = 128
DEVICES = 128
FINAL_ROWS = 16
MESSAGE = 24
SLICE = 12
STRIPS = 55
HALF = 27
TAIL = 56
DEAD = 64
AXES = ("row", "col")
PARAMS = pltpu.CompilerParams(vmem_limit_bytes=48 * 1024 * 1024)


def lane_index(shape):
    return lax.broadcasted_iota(jnp.int32, shape, len(shape) - 1)


def send_kernel(count_ref, final_ref, initial_ref, pf_ref, pi_ref, mf_ref, mi_ref, out_ref, maps, wide):
    maps[...] = jnp.full(maps.shape, -1, jnp.int32)
    maps[0:4, 0:440] = mf_ref[0]
    maps[4:6, 0:440] = mi_ref[0]
    slot = lane_index((1, LANES))
    q = pf_ref[0]
    s = pi_ref[0]
    q_code = jnp.where(slot < count_ref[0, 0], (q & 3) * 8 + (q >> 2), DEAD).astype(jnp.float32)
    s_code = ((s & 1) * LANES + (s >> 1) * 8).astype(jnp.float32)
    q_code = jnp.broadcast_to(q_code, (8, LANES))
    s_code = jnp.broadcast_to(s_code, (8, LANES))
    info = [pltpu.roll(q_code, 64, 1), q_code, pltpu.roll(s_code, 64, 1), s_code]
    upper = lane_index((LANES, LANES)) >= 64
    for j in range(6):
        block = final_ref[0, j] if j < 4 else initial_ref[0, j - 4]
        stored = lax.broadcasted_iota(jnp.int32, (440, 512), 0)
        pick = jnp.where(stored == maps[j : j + 1, :], 1.0, 0.0).astype(jnp.bfloat16)
        ordered = jnp.dot(block, pick, preferred_element_type=jnp.float32)
        for chunk in range(4):
            part = ordered[:, chunk * LANES : (chunk + 1) * LANES]
            if chunk == 3 and j < 4:
                part = jnp.where(upper, jnp.broadcast_to(info[j][0:1], (LANES, LANES)), part)
            wide[pl.ds(j * 4 + chunk, DEVICES, stride=MESSAGE), :] = part
    out_ref[...] = wide[...].astype(jnp.bfloat16)


def density_kernel(in_ref, out_ref, wide, pairs, final, initial, full):
    wide[...] = in_ref[...].astype(jnp.float32)

    def rows(r):
        return wide[pl.ds(r, DEVICES, stride=MESSAGE), :]

    lower = lane_index((LANES, LANES)) < 64
    codes = [
        jnp.where(lower, pltpu.roll(rows(3 + 8 * k), 64, 1), rows(7 + 8 * k)).astype(jnp.int32) for k in range(2)
    ]
    pairs[0:LANES, :] = codes[0]
    pairs[LANES:, :] = codes[1] + (lax.broadcasted_iota(jnp.int32, (LANES, LANES), 0) & 7)

    for j in range(4):
        for chunk in range(4):
            final[j * LANES : (j + 1) * LANES, chunk * LANES : (chunk + 1) * LANES] = rows(j * 4 + chunk).astype(jnp.bfloat16)
    for j in range(2):
        for chunk in range(4):
            part = rows(FINAL_ROWS + j * 4 + chunk).astype(jnp.bfloat16)
            initial[j * LANES : (j + 1) * LANES, chunk * LANES : (chunk + 1) * LANES] = part
            initial[(2 + j) * LANES : (3 + j) * LANES, chunk * LANES : (chunk + 1) * LANES] = part

    def count(r, carry):
        q = pairs[pl.ds(pl.multiple_of(r * 8, 8), 8), :]
        s = pairs[pl.ds(pl.multiple_of(LANES + r * 8, 8), 8), :]
        final_is = lax.broadcasted_iota(jnp.int32, (32, LANES), 0)
        initial_is = lax.broadcasted_iota(jnp.int32, (256, LANES), 0)
        left = jnp.concatenate([jnp.where(final_is == q[c : c + 1], 1.0, 0.0) for c in range(8)], axis=1)
        right = jnp.concatenate([jnp.where(initial_is == s[c : c + 1], 1.0, 0.0) for c in range(8)], axis=1)
        met = lax.dot_general(
            left.astype(jnp.bfloat16),
            right.astype(jnp.bfloat16),
            (((1,), (1,)), ((), ())),
            preferred_element_type=jnp.float32,
        )
        for j in range(4):
            full[pl.ds(pl.multiple_of(j * LANES + r * 8, 8), 8), 0:256] = met[j * 8 : (j + 1) * 8]
        return carry

    lax.fori_loop(0, 16, count, 0)
    met = full[:, 0:256].astype(jnp.bfloat16)
    across = (((0,), (0,)), ((), ()))
    summed = lax.dot_general(met, final[...], across, preferred_element_type=jnp.float32)
    high = summed.astype(jnp.bfloat16)
    low = (summed - high.astype(jnp.float32)).astype(jnp.bfloat16)
    full[...] = lax.dot_general(
        jnp.concatenate([high, low], axis=0), initial[...], across, preferred_element_type=jnp.float32
    )

    lane = lane_index((8, LANES))

    def tile(e, chunk):
        return full[e * 8 : (e + 1) * 8, chunk * LANES : (chunk + 1) * LANES]

    for e in range(STRIPS):
        for chunk in range(3):
            t = e * 3 + chunk
            out_ref[t * 8 : (t + 1) * 8, :] = tile(e, chunk)
    last = tile(STRIPS - 1, 3)
    for e in range(HALF):
        t = STRIPS * 3 + e
        packed = jnp.where(lane < 64, tile(e, 3), pltpu.roll(tile(e + HALF, 3), 64, 1))
        if e < 7:
            packed = jnp.where((lane >= TAIL) & (lane < 64), pltpu.roll(last, TAIL - 8 * e, 1), packed)
        out_ref[t * 8 : (t + 1) * 8, :] = packed


def sum_kernel(in_ref, out_ref):
    total = in_ref[0:24, :]
    for d in range(1, DEVICES // 2):
        total = total + in_ref[d * 24 : (d + 1) * 24, :]
    own = total[0:SLICE] + total[SLICE:24]
    twice = jnp.concatenate([own, own], axis=0)
    for d in range(DEVICES // 2):
        out_ref[d * 24 : (d + 1) * 24, :] = twice


def place_kernel(in_ref, out_ref):
    def tile(t):
        return in_ref[t * 8 : (t + 1) * 8, :]

    lane = lane_index((8, LANES))
    for e in range(STRIPS):
        for chunk in range(3):
            out_ref[e * 8 : (e + 1) * 8, chunk * LANES : (chunk + 1) * LANES] = tile(e * 3 + chunk)
        if e < HALF:
            strip = tile(STRIPS * 3 + e)
        elif e < STRIPS - 1:
            strip = pltpu.roll(tile(STRIPS * 3 + e - HALF), 64, 1)
        else:
            strip = jnp.zeros((8, LANES), jnp.float32)
            for k in range(7):
                piece = pltpu.roll(tile(STRIPS * 3 + k), (8 * k - TAIL) % LANES, 1)
                strip = jnp.where((lane >= 8 * k) & (lane < 8 * k + 8), piece, strip)
        out_ref[e * 8 : (e + 1) * 8, 3 * LANES : 440] = strip[:, 0:TAIL]


def exchange(x, shape):
    return lax.all_to_all(x.reshape((DEVICES,) + shape), AXES, 0, 0, tiled=True).reshape(x.shape)


def shards(final_amp, initial_amp, pair_final, pair_initial, map_final, map_initial, counts):
    vmem = pl.BlockSpec(memory_space=pltpu.VMEM)
    smem = pl.BlockSpec(memory_space=pltpu.SMEM)
    f32, bf16 = jnp.float32, jnp.bfloat16
    messages = pl.pallas_call(
        send_kernel,
        out_shape=jax.ShapeDtypeStruct((DEVICES * MESSAGE, LANES), bf16),
        in_specs=[smem] + [vmem] * 6,
        out_specs=vmem,
        scratch_shapes=[pltpu.VMEM((8, 512), jnp.int32), pltpu.VMEM((DEVICES * MESSAGE, LANES), f32)],
        compiler_params=PARAMS,
    )(counts, final_amp, initial_amp, pair_final, pair_initial, map_final, map_initial)
    received = exchange(messages, (MESSAGE, LANES))
    share = pl.pallas_call(
        density_kernel,
        out_shape=jax.ShapeDtypeStruct((DEVICES * SLICE, LANES), f32),
        in_specs=[vmem],
        out_specs=vmem,
        scratch_shapes=[
            pltpu.VMEM((DEVICES * MESSAGE, LANES), f32),
            pltpu.VMEM((2 * LANES, LANES), jnp.int32),
            pltpu.VMEM((512, 512), bf16),
            pltpu.VMEM((512, 512), bf16),
            pltpu.VMEM((512, 512), f32),
        ],
        compiler_params=PARAMS,
    )(received)
    shares = exchange(share, (3, 4, LANES))
    copies = pl.pallas_call(
        sum_kernel,
        out_shape=jax.ShapeDtypeStruct((DEVICES * SLICE, LANES), f32),
        in_specs=[vmem],
        out_specs=vmem,
        compiler_params=PARAMS,
    )(shares)
    slices = exchange(copies, (3, 4, LANES))
    return pl.pallas_call(
        place_kernel,
        out_shape=jax.ShapeDtypeStruct((440, 440), f32),
        in_specs=[vmem],
        out_specs=vmem,
        compiler_params=PARAMS,
    )(slices)


def solution(mesh):
    placed = (
        P("row", "col", None, None),
        P("col", "row", None, None),
        P("row", "col", None),
        P("row", "col", None),
        P("row", "col", None),
        P("col", "row", None),
        P("row", "col"),
    )
    return jax.shard_map(shards, mesh=mesh, in_specs=placed, out_specs=P(), check_vma=False)
```

```python
import jax
import jax.numpy as jnp
from jax import lax
from jax.experimental import pallas as pl
from jax.experimental.pallas import tpu as pltpu
from jax.sharding import Mesh
from jax.sharding import PartitionSpec as P

LANES = 128
DEVICES = 128
CHIPS = 64
FINAL_ROWS = 16
MESSAGE = 24
SLICE = 12
TILES = 192
STRIPS = 55
HALF = 27
TAIL = 56
DEAD = 64
ALL = ("x", "y_hi", "core", "y_lo", "z")
ACROSS_CHIPS = ("x", "y_hi", "y_lo", "z")
PARAMS = pltpu.CompilerParams(vmem_limit_bytes=48 * 1024 * 1024)


def lane_index(shape):
    return lax.broadcasted_iota(jnp.int32, shape, len(shape) - 1)


def send_kernel(count_ref, final_ref, initial_ref, pf_ref, pi_ref, mf_ref, mi_ref, out_ref, maps, wide):
    maps[...] = jnp.full(maps.shape, -1, jnp.int32)
    maps[0:4, 0:440] = mf_ref[0]
    maps[4:6, 0:440] = mi_ref[0]
    slot = lane_index((1, LANES))
    q = pf_ref[0]
    s = pi_ref[0]
    q_code = jnp.where(slot < count_ref[0, 0], (q & 3) * 8 + (q >> 2), DEAD).astype(jnp.float32)
    s_code = ((s & 1) * LANES + (s >> 1) * 8).astype(jnp.float32)
    q_code = jnp.broadcast_to(q_code, (8, LANES))
    s_code = jnp.broadcast_to(s_code, (8, LANES))
    info = [pltpu.roll(q_code, 64, 1), q_code, pltpu.roll(s_code, 64, 1), s_code]
    upper = lane_index((LANES, LANES)) >= 64
    for j in range(6):
        block = final_ref[0, j] if j < 4 else initial_ref[0, j - 4]
        stored = lax.broadcasted_iota(jnp.int32, (440, 512), 0)
        pick = jnp.where(stored == maps[j : j + 1, :], 1.0, 0.0).astype(jnp.bfloat16)
        ordered = lax.dot_general(block, pick, (((0,), (0,)), ((), ())), preferred_element_type=jnp.float32)
        for chunk in range(4):
            part = ordered[:, chunk * LANES : (chunk + 1) * LANES]
            if chunk == 3 and j < 4:
                part = jnp.where(upper, jnp.broadcast_to(info[j][0:1], (LANES, LANES)), part)
            wide[pl.ds(j * 4 + chunk, DEVICES, stride=MESSAGE), :] = part
    out_ref[...] = wide[...].astype(jnp.bfloat16)


def density_kernel(in_ref, keep_ref, give_ref, wide, pairs, final, initial, full):
    wide[...] = in_ref[...].astype(jnp.float32)

    def rows(r):
        return wide[pl.ds(r, DEVICES, stride=MESSAGE), :]

    lower = lane_index((LANES, LANES)) < 64
    codes = [
        jnp.where(lower, pltpu.roll(rows(3 + 8 * k), 64, 1), rows(7 + 8 * k)).astype(jnp.int32) for k in range(2)
    ]
    pairs[0:LANES, :] = codes[0]
    pairs[LANES:, :] = codes[1] + (lax.broadcasted_iota(jnp.int32, (LANES, LANES), 0) & 7)

    for j in range(4):
        for chunk in range(4):
            final[j * LANES : (j + 1) * LANES, chunk * LANES : (chunk + 1) * LANES] = rows(j * 4 + chunk).astype(jnp.bfloat16)
    for j in range(2):
        for chunk in range(4):
            part = rows(FINAL_ROWS + j * 4 + chunk).astype(jnp.bfloat16)
            initial[j * LANES : (j + 1) * LANES, chunk * LANES : (chunk + 1) * LANES] = part
            initial[(2 + j) * LANES : (3 + j) * LANES, chunk * LANES : (chunk + 1) * LANES] = part

    final_is = lax.broadcasted_iota(jnp.int32, (32, LANES), 0)
    initial_is = lax.broadcasted_iota(jnp.int32, (256, LANES), 0)
    for r in range(16):
        q = pairs[r * 8 : r * 8 + 8, :]
        s = pairs[LANES + r * 8 : LANES + r * 8 + 8, :]
        left = jnp.concatenate([jnp.where(final_is == q[c : c + 1], 1.0, 0.0) for c in range(8)], axis=1)
        right = jnp.concatenate([jnp.where(initial_is == s[c : c + 1], 1.0, 0.0) for c in range(8)], axis=1)
        met = lax.dot_general(
            left.astype(jnp.bfloat16),
            right.astype(jnp.bfloat16),
            (((1,), (1,)), ((), ())),
            preferred_element_type=jnp.float32,
        )
        for j in range(4):
            full[j * LANES + r * 8 : j * LANES + r * 8 + 8, 0:256] = met[j * 8 : (j + 1) * 8]

    met = full[:, 0:256].astype(jnp.bfloat16)
    across = (((0,), (0,)), ((), ()))
    summed = lax.dot_general(met, final[...], across, preferred_element_type=jnp.float32)
    high = summed.astype(jnp.bfloat16)
    low = (summed - high.astype(jnp.float32)).astype(jnp.bfloat16)
    full[...] = lax.dot_general(
        jnp.concatenate([high, low], axis=0), initial[...], across, preferred_element_type=jnp.float32
    )

    lane = lane_index((8, LANES))

    def tile(e, chunk):
        return full[e * 8 : (e + 1) * 8, chunk * LANES : (chunk + 1) * LANES]

    def packed(t):
        if t < STRIPS * 3:
            return tile(t // 3, t % 3)
        e = t - STRIPS * 3
        two = jnp.where(lane < 64, tile(e, 3), pltpu.roll(tile(e + HALF, 3), 64, 1))
        if e < 7:
            two = jnp.where((lane >= TAIL) & (lane < 64), pltpu.roll(tile(STRIPS - 1, 3), TAIL - 8 * e, 1), two)
        return two

    def split(first, second):
        for t in range(TILES // 2):
            first[t * 8 : (t + 1) * 8, :] = packed(t)
            second[t * 8 : (t + 1) * 8, :] = packed(t + TILES // 2)

    core = lax.axis_index("core")
    pl.when(core == 0)(lambda: split(keep_ref, give_ref))
    pl.when(core == 1)(lambda: split(give_ref, keep_ref))


def add_kernel(a_ref, b_ref, out_ref):
    out_ref[...] = a_ref[...] + b_ref[...]


def sum_kernel(in_ref, out_ref):
    total = in_ref[0:24, :]
    for d in range(1, CHIPS // 2):
        total = total + in_ref[d * 24 : (d + 1) * 24, :]
    own = total[0:SLICE] + total[SLICE:24]
    twice = jnp.concatenate([own, own], axis=0)
    for d in range(CHIPS // 2):
        out_ref[d * 24 : (d + 1) * 24, :] = twice


def place_kernel(kept_ref, given_ref, out_ref):
    lane = lane_index((8, LANES))

    def place(first, second):
        def tile(t):
            half, t = (first, t) if t < TILES // 2 else (second, t - TILES // 2)
            return half[t * 8 : (t + 1) * 8, :]

        for e in range(STRIPS):
            for chunk in range(3):
                out_ref[e * 8 : (e + 1) * 8, chunk * LANES : (chunk + 1) * LANES] = tile(e * 3 + chunk)
            if e < HALF:
                strip = tile(STRIPS * 3 + e)
            elif e < STRIPS - 1:
                strip = pltpu.roll(tile(STRIPS * 3 + e - HALF), 64, 1)
            else:
                strip = jnp.zeros((8, LANES), jnp.float32)
                for k in range(7):
                    piece = pltpu.roll(tile(STRIPS * 3 + k), (8 * k - TAIL) % LANES, 1)
                    strip = jnp.where((lane >= 8 * k) & (lane < 8 * k + 8), piece, strip)
            out_ref[e * 8 : (e + 1) * 8, 3 * LANES : 440] = strip[:, 0:TAIL]

    core = lax.axis_index("core")
    pl.when(core == 0)(lambda: place(kept_ref, given_ref))
    pl.when(core == 1)(lambda: place(given_ref, kept_ref))


def exchange(x, axes, shape):
    return lax.all_to_all(x.reshape(shape), axes, 0, 0, tiled=True).reshape(x.shape)


def to_other_core(x):
    return lax.ppermute(x, "core", [(0, 1), (1, 0)])


def shards(final_amp, initial_amp, pair_final, pair_initial, map_final, map_initial, counts):
    vmem = pl.BlockSpec(memory_space=pltpu.VMEM)
    smem = pl.BlockSpec(memory_space=pltpu.SMEM)
    f32, bf16 = jnp.float32, jnp.bfloat16
    half = jax.ShapeDtypeStruct((CHIPS * SLICE, LANES), f32)

    def call(kernel, out_shape, n, scratch=()):
        several = isinstance(out_shape, list)
        return pl.pallas_call(
            kernel,
            out_shape=out_shape,
            in_specs=[vmem] * n,
            out_specs=[vmem] * len(out_shape) if several else vmem,
            scratch_shapes=list(scratch),
            compiler_params=PARAMS,
        )

    messages = pl.pallas_call(
        send_kernel,
        out_shape=jax.ShapeDtypeStruct((DEVICES * MESSAGE, LANES), bf16),
        in_specs=[smem] + [vmem] * 6,
        out_specs=vmem,
        scratch_shapes=[pltpu.VMEM((8, 512), jnp.int32), pltpu.VMEM((DEVICES * MESSAGE, LANES), f32)],
        compiler_params=PARAMS,
    )(
        counts,
        jnp.swapaxes(final_amp, 2, 3),
        jnp.swapaxes(initial_amp, 2, 3),
        pair_final,
        pair_initial,
        map_final,
        map_initial,
    )
    received = exchange(messages, ALL, (DEVICES, MESSAGE, LANES))
    keep, give = call(
        density_kernel,
        [half, half],
        1,
        [
            pltpu.VMEM((DEVICES * MESSAGE, LANES), f32),
            pltpu.VMEM((2 * LANES, LANES), jnp.int32),
            pltpu.VMEM((512, 512), bf16),
            pltpu.VMEM((512, 512), bf16),
            pltpu.VMEM((512, 512), f32),
        ],
    )(received)
    share = call(add_kernel, half, 2)(keep, to_other_core(give))
    shares = exchange(share, ACROSS_CHIPS, (CHIPS, 3, 4, LANES))
    copies = call(sum_kernel, half, 1)(shares)
    slices = exchange(copies, ACROSS_CHIPS, (CHIPS, 3, 4, LANES))
    return call(place_kernel, jax.ShapeDtypeStruct((440, 440), f32), 2)(slices, to_other_core(slices))


def solution(mesh):
    cores = Mesh(mesh.devices.reshape(4, 2, 2, 2, 4), ALL)
    row, col = ("x", "y_hi", "core"), ("y_lo", "z")
    placed = (
        P(row, col, None, None),
        P(col, row, None, None),
        P(row, col, None),
        P(row, col, None),
        P(row, col, None),
        P(col, row, None),
        P(row, col),
    )
    return jax.shard_map(shards, mesh=cores, in_specs=placed, out_specs=P(), check_vma=False)
```

```python
import jax
import jax.numpy as jnp
from jax import lax
from jax.experimental import pallas as pl
from jax.experimental.pallas import tpu as pltpu
from jax.sharding import Mesh
from jax.sharding import PartitionSpec as P

LANES = 128
DEVICES = 128
CHIPS = 64
FINAL_ROWS = 16
MESSAGE = 24
SLICE = 12
TILES = 192
STRIPS = 55
HALF = 27
TAIL = 56
DEAD = 64
ALL = ("x", "y_hi", "core", "y_lo", "z")
ACROSS_CHIPS = ("x", "y_hi", "y_lo", "z")
PARAMS = pltpu.CompilerParams(vmem_limit_bytes=48 * 1024 * 1024)


def lane_index(shape):
    return lax.broadcasted_iota(jnp.int32, shape, len(shape) - 1)


def send_kernel(counts, finals, initials, pairs_final, pairs_initial, maps_final, maps_initial, out_ref, *scratch):
    count, blocks, pf, pi, mf, mi, maps, wide, arrived = scratch
    small = [(counts, count), (pairs_final, pf), (pairs_initial, pi), (maps_final, mf), (maps_initial, mi)]
    large = [(finals.at[0, j], blocks.at[j]) for j in range(4)] + [(initials.at[0, j], blocks.at[4 + j]) for j in range(2)]
    copies = [pltpu.make_async_copy(a, b, arrived.at[n]) for n, (a, b) in enumerate(small + large)]
    for copy in copies:
        copy.start()
    maps[...] = jnp.full(maps.shape, -1, jnp.int32)
    for copy in copies[: len(small)]:
        copy.wait()
    maps[0:4, 0:440] = mf[0]
    maps[4:6, 0:440] = mi[0]
    slot = lane_index((1, LANES))
    q = pf[0]
    s = pi[0]
    q_code = jnp.where(slot < count[...], (q & 3) * 8 + (q >> 2), DEAD).astype(jnp.float32)
    s_code = ((s & 1) * 16 + (s >> 1)).astype(jnp.float32)
    q_code = jnp.broadcast_to(q_code, (8, LANES))
    s_code = jnp.broadcast_to(s_code, (8, LANES))
    info = [pltpu.roll(q_code, 64, 1), q_code, pltpu.roll(s_code, 64, 1), s_code]
    upper = lane_index((LANES, LANES)) >= 64
    for j in range(6):
        stored = lax.broadcasted_iota(jnp.int32, (440, 512), 0)
        pick = jnp.where(stored == maps[j : j + 1, :], 1.0, 0.0).astype(jnp.bfloat16)
        copies[len(small) + j].wait()
        ordered = lax.dot_general(blocks[j], pick, (((0,), (0,)), ((), ())), preferred_element_type=jnp.float32)
        for chunk in range(4):
            part = ordered[:, chunk * LANES : (chunk + 1) * LANES]
            if chunk == 3 and j < 4:
                part = jnp.where(upper, jnp.broadcast_to(info[j][0:1], (LANES, LANES)), part)
            wide[pl.ds(j * 4 + chunk, DEVICES, stride=MESSAGE), :] = part
    out_ref[...] = wide[...].astype(jnp.bfloat16)


def density_kernel(in_ref, keep_ref, give_ref, wide, pairs, final, initial, met, full):
    wide[...] = in_ref[...].astype(jnp.float32)

    def rows(r):
        return wide[pl.ds(r, DEVICES, stride=MESSAGE), :]

    lower = lane_index((LANES, LANES)) < 64
    for k in range(2):
        pairs[k * LANES : (k + 1) * LANES, :] = jnp.where(lower, pltpu.roll(rows(3 + 8 * k), 64, 1), rows(7 + 8 * k))

    for r in range(16):
        for chunk in range(4):
            part = [wide[pl.ds(r * 8 * MESSAGE + j * 4 + chunk, 8, stride=MESSAGE), :] for j in range(4)]
            final[r * 32 : (r + 1) * 32, chunk * LANES : (chunk + 1) * LANES] = jnp.concatenate(part, axis=0).astype(jnp.bfloat16)
    for j in range(2):
        for chunk in range(4):
            part = rows(FINAL_ROWS + j * 4 + chunk).astype(jnp.bfloat16)
            initial[j * LANES : (j + 1) * LANES, chunk * LANES : (chunk + 1) * LANES] = part
            initial[(2 + j) * LANES : (3 + j) * LANES, chunk * LANES : (chunk + 1) * LANES] = part

    code = lax.broadcasted_iota(jnp.int32, (32, LANES), 0).astype(jnp.float32)

    def one_hot(slots):
        return jnp.where(code == slots, 1.0, 0.0).astype(jnp.bfloat16)

    for c in range(8):
        for g in range(4):
            cells = []
            for d in range(g * 32 + c, g * 32 + 32, 8):
                cells.append(
                    lax.dot_general(
                        one_hot(pairs[LANES + d : LANES + d + 1, :]),
                        one_hot(pairs[d : d + 1, :]),
                        (((1,), (1,)), ((), ())),
                        preferred_element_type=jnp.float32,
                    )
                )
            cells = jnp.concatenate(cells, axis=1)
            for j in range(2):
                met[pl.ds(g * 256 + j * LANES + c, 16, stride=8), :] = cells[j * 16 : (j + 1) * 16]

    times = jnp.concatenate([met[g * 256 : (g + 1) * 256, :].astype(jnp.bfloat16) for g in range(4)], axis=1)
    summed = jnp.dot(times, final[...], preferred_element_type=jnp.float32)
    high = summed.astype(jnp.bfloat16)
    low = (summed - high.astype(jnp.float32)).astype(jnp.bfloat16)
    full[...] = lax.dot_general(
        jnp.concatenate([high, low], axis=0),
        initial[...],
        (((0,), (0,)), ((), ())),
        preferred_element_type=jnp.float32,
    )

    lane = lane_index((8, LANES))

    def tile(e, chunk):
        return full[e * 8 : (e + 1) * 8, chunk * LANES : (chunk + 1) * LANES]

    def packed(t):
        if t < STRIPS * 3:
            return tile(t // 3, t % 3)
        e = t - STRIPS * 3
        two = jnp.where(lane < 64, tile(e, 3), pltpu.roll(tile(e + HALF, 3), 64, 1))
        if e < 7:
            two = jnp.where((lane >= TAIL) & (lane < 64), pltpu.roll(tile(STRIPS - 1, 3), TAIL - 8 * e, 1), two)
        return two

    def split(first, second):
        for t in range(TILES // 2):
            first[t * 8 : (t + 1) * 8, :] = packed(t)
            second[t * 8 : (t + 1) * 8, :] = packed(t + TILES // 2)

    core = lax.axis_index("core")
    pl.when(core == 0)(lambda: split(keep_ref, give_ref))
    pl.when(core == 1)(lambda: split(give_ref, keep_ref))


def add_kernel(a_ref, b_ref, out_ref):
    out_ref[...] = a_ref[...] + b_ref[...]


def sum_kernel(in_ref, out_ref):
    total = in_ref[0:24, :]
    for d in range(1, CHIPS // 2):
        total = total + in_ref[d * 24 : (d + 1) * 24, :]
    own = total[0:SLICE] + total[SLICE:24]
    twice = jnp.concatenate([own, own], axis=0)
    for d in range(CHIPS // 2):
        out_ref[d * 24 : (d + 1) * 24, :] = twice


def place_kernel(kept_ref, given_ref, out_hbm, out_ref, sent):
    lane = lane_index((8, LANES))
    copies = [
        pltpu.make_async_copy(out_ref.at[n * 88 : (n + 1) * 88], out_hbm.at[n * 88 : (n + 1) * 88], sent.at[n]) for n in range(5)
    ]

    def place(first, second):
        def tile(t):
            half, t = (first, t) if t < TILES // 2 else (second, t - TILES // 2)
            return half[t * 8 : (t + 1) * 8, :]

        for e in range(STRIPS):
            for chunk in range(3):
                out_ref[e * 8 : (e + 1) * 8, chunk * LANES : (chunk + 1) * LANES] = tile(e * 3 + chunk)
            if e < HALF:
                strip = tile(STRIPS * 3 + e)
            elif e < STRIPS - 1:
                strip = pltpu.roll(tile(STRIPS * 3 + e - HALF), 64, 1)
            else:
                strip = jnp.zeros((8, LANES), jnp.float32)
                for k in range(7):
                    piece = pltpu.roll(tile(STRIPS * 3 + k), (8 * k - TAIL) % LANES, 1)
                    strip = jnp.where((lane >= 8 * k) & (lane < 8 * k + 8), piece, strip)
            out_ref[e * 8 : (e + 1) * 8, 3 * LANES : 440] = strip[:, 0:TAIL]
            if e % 11 == 10:
                copies[e // 11].start()

    core = lax.axis_index("core")
    pl.when(core == 0)(lambda: place(kept_ref, given_ref))
    pl.when(core == 1)(lambda: place(given_ref, kept_ref))
    for copy in copies:
        copy.wait()


def exchange(x, axes, shape):
    return lax.all_to_all(x.reshape(shape), axes, 0, 0, tiled=True).reshape(x.shape)


def to_other_core(x):
    return lax.ppermute(x, "core", [(0, 1), (1, 0)])


def shards(final_amp, initial_amp, pair_final, pair_initial, map_final, map_initial, counts):
    vmem = pl.BlockSpec(memory_space=pltpu.VMEM)
    f32, bf16 = jnp.float32, jnp.bfloat16
    half = jax.ShapeDtypeStruct((CHIPS * SLICE, LANES), f32)

    def call(kernel, out_shape, n, scratch=()):
        several = isinstance(out_shape, list)
        return pl.pallas_call(
            kernel,
            out_shape=out_shape,
            in_specs=[vmem] * n,
            out_specs=[vmem] * len(out_shape) if several else vmem,
            scratch_shapes=list(scratch),
            compiler_params=PARAMS,
        )

    messages = pl.pallas_call(
        send_kernel,
        out_shape=jax.ShapeDtypeStruct((DEVICES * MESSAGE, LANES), bf16),
        in_specs=[pl.BlockSpec(memory_space=pltpu.HBM)] * 7,
        out_specs=vmem,
        scratch_shapes=[
            pltpu.VMEM((1, 1), jnp.int32),
            pltpu.VMEM((6, 440, LANES), bf16),
            pltpu.VMEM((1, 1, LANES), jnp.int32),
            pltpu.VMEM((1, 1, LANES), jnp.int32),
            pltpu.VMEM((1, 4, 440), jnp.int32),
            pltpu.VMEM((1, 2, 440), jnp.int32),
            pltpu.VMEM((8, 512), jnp.int32),
            pltpu.VMEM((DEVICES * MESSAGE, LANES), f32),
            pltpu.SemaphoreType.DMA((11,)),
        ],
        compiler_params=pltpu.CompilerParams(vmem_limit_bytes=60 * 1024 * 1024),
    )(
        counts,
        jnp.swapaxes(final_amp, 2, 3),
        jnp.swapaxes(initial_amp, 2, 3),
        pair_final,
        pair_initial,
        map_final,
        map_initial,
    )
    received = exchange(messages, ALL, (DEVICES, MESSAGE, LANES))
    keep, give = call(
        density_kernel,
        [half, half],
        1,
        [
            pltpu.VMEM((DEVICES * MESSAGE, LANES), f32),
            pltpu.VMEM((2 * LANES, LANES), f32),
            pltpu.VMEM((512, 512), bf16),
            pltpu.VMEM((512, 512), bf16),
            pltpu.VMEM((4 * 256, LANES), f32),
            pltpu.VMEM((512, 512), f32),
        ],
    )(received)
    share = call(add_kernel, half, 2)(keep, to_other_core(give))
    shares = exchange(share, ACROSS_CHIPS, (CHIPS, 3, 4, LANES))
    copies = call(sum_kernel, half, 1)(shares)
    slices = exchange(copies, ACROSS_CHIPS, (CHIPS, 3, 4, LANES))
    return pl.pallas_call(
        place_kernel,
        out_shape=jax.ShapeDtypeStruct((440, 440), f32),
        in_specs=[vmem] * 2,
        out_specs=pl.BlockSpec(memory_space=pltpu.HBM),
        scratch_shapes=[pltpu.VMEM((440, 440), f32), pltpu.SemaphoreType.DMA((5,))],
        compiler_params=PARAMS,
    )(slices, to_other_core(slices))


def solution(mesh):
    cores = Mesh(mesh.devices.reshape(4, 2, 2, 2, 4), ALL)
    row, col = ("x", "y_hi", "core"), ("y_lo", "z")
    placed = (
        P(row, col, None, None),
        P(col, row, None, None),
        P(row, col, None),
        P(row, col, None),
        P(row, col, None),
        P(col, row, None),
        P(row, col),
    )
    return jax.shard_map(shards, mesh=cores, in_specs=placed, out_specs=P(), check_vma=False)
```

```python
import jax
import jax.numpy as jnp
from jax import lax
from jax.experimental import pallas as pl
from jax.experimental.pallas import tpu as pltpu
from jax.sharding import Mesh
from jax.sharding import PartitionSpec as P

LANES = 128
DEVICES = 128
CHIPS = 64
FINAL_ROWS = 16
MESSAGE = 24
SLICE = 12
TILES = 192
STRIPS = 55
HALF = 27
TAIL = 56
DEAD = 64
ALL = ("x", "y_hi", "core", "y_lo", "z")
ACROSS_CHIPS = ("x", "y_hi", "y_lo", "z")
PARAMS = pltpu.CompilerParams(vmem_limit_bytes=48 * 1024 * 1024)


def lane_index(shape):
    return lax.broadcasted_iota(jnp.int32, shape, len(shape) - 1)


def send_kernel(counts, finals, initials, pairs_final, pairs_initial, maps_final, maps_initial, out_ref, *scratch):
    blocks, pf, pi, mf, mi, maps, wide, arrived = scratch
    pairs = [
        (finals.at[0], blocks.at[0:4]),
        (initials.at[0], blocks.at[4:6]),
        (maps_final, mf),
        (maps_initial, mi),
        (pairs_final, pf),
        (pairs_initial, pi),
    ]
    copies = [pltpu.make_async_copy(there, here, arrived.at[n]) for n, (there, here) in enumerate(pairs)]
    for copy in copies:
        copy.start()
    maps[...] = jnp.full(maps.shape, -1, jnp.int32)
    for copy in copies:
        copy.wait()
    maps[0:4, 0:440] = mf[0]
    maps[4:6, 0:440] = mi[0]
    slot = lane_index((1, LANES))
    q = pf[0]
    s = pi[0]
    q_code = jnp.where(slot < counts[0, 0], (q & 3) * 8 + (q >> 2), DEAD).astype(jnp.float32)
    s_code = ((s & 1) * 16 + (s >> 1)).astype(jnp.float32)
    q_code = jnp.broadcast_to(q_code, (8, LANES))
    s_code = jnp.broadcast_to(s_code, (8, LANES))
    info = [pltpu.roll(q_code, 64, 1), q_code, pltpu.roll(s_code, 64, 1), s_code]
    upper = lane_index((LANES, LANES)) >= 64
    for j in range(6):
        stored = lax.broadcasted_iota(jnp.int32, (440, 512), 0)
        pick = jnp.where(stored == maps[j : j + 1, :], 1.0, 0.0).astype(jnp.bfloat16)
        ordered = lax.dot_general(blocks[j], pick, (((0,), (0,)), ((), ())), preferred_element_type=jnp.float32)
        for chunk in range(4):
            part = ordered[:, chunk * LANES : (chunk + 1) * LANES]
            if chunk == 3 and j < 4:
                part = jnp.where(upper, jnp.broadcast_to(info[j][0:1], (LANES, LANES)), part)
            wide[pl.ds(j * 4 + chunk, DEVICES, stride=MESSAGE), :] = part
    out_ref[...] = wide[...].astype(jnp.bfloat16)


def density_kernel(in_ref, keep_ref, give_ref, wide, pairs, final, initial, met, full):
    wide[...] = in_ref[...].astype(jnp.float32)

    def rows(r):
        return wide[pl.ds(r, DEVICES, stride=MESSAGE), :]

    lower = lane_index((LANES, LANES)) < 64
    for k in range(2):
        pairs[k * LANES : (k + 1) * LANES, :] = jnp.where(lower, pltpu.roll(rows(3 + 8 * k), 64, 1), rows(7 + 8 * k))

    for r in range(16):
        for chunk in range(4):
            part = [wide[pl.ds(r * 8 * MESSAGE + j * 4 + chunk, 8, stride=MESSAGE), :] for j in range(4)]
            final[r * 32 : (r + 1) * 32, chunk * LANES : (chunk + 1) * LANES] = jnp.concatenate(part, axis=0).astype(jnp.bfloat16)
    for j in range(2):
        for chunk in range(4):
            part = rows(FINAL_ROWS + j * 4 + chunk).astype(jnp.bfloat16)
            initial[j * LANES : (j + 1) * LANES, chunk * LANES : (chunk + 1) * LANES] = part
            initial[(2 + j) * LANES : (3 + j) * LANES, chunk * LANES : (chunk + 1) * LANES] = part

    code = lax.broadcasted_iota(jnp.int32, (32, LANES), 0).astype(jnp.float32)

    def one_hot(slots):
        return jnp.where(code == slots, 1.0, 0.0).astype(jnp.bfloat16)

    for c in range(8):
        for g in range(4):
            cells = []
            for d in range(g * 32 + c, g * 32 + 32, 8):
                cells.append(
                    lax.dot_general(
                        one_hot(pairs[LANES + d : LANES + d + 1, :]),
                        one_hot(pairs[d : d + 1, :]),
                        (((1,), (1,)), ((), ())),
                        preferred_element_type=jnp.float32,
                    )
                )
            cells = jnp.concatenate(cells, axis=1)
            for j in range(2):
                met[pl.ds(g * 256 + j * LANES + c, 16, stride=8), :] = cells[j * 16 : (j + 1) * 16]

    times = jnp.concatenate([met[g * 256 : (g + 1) * 256, :].astype(jnp.bfloat16) for g in range(4)], axis=1)
    summed = jnp.dot(times, final[...], preferred_element_type=jnp.float32)
    high = summed.astype(jnp.bfloat16)
    low = (summed - high.astype(jnp.float32)).astype(jnp.bfloat16)
    full[...] = lax.dot_general(
        jnp.concatenate([high, low], axis=0),
        initial[...],
        (((0,), (0,)), ((), ())),
        preferred_element_type=jnp.float32,
    )

    lane = lane_index((8, LANES))

    def tile(e, chunk):
        return full[e * 8 : (e + 1) * 8, chunk * LANES : (chunk + 1) * LANES]

    def packed(t):
        if t < STRIPS * 3:
            return tile(t // 3, t % 3)
        e = t - STRIPS * 3
        two = jnp.where(lane < 64, tile(e, 3), pltpu.roll(tile(e + HALF, 3), 64, 1))
        if e < 7:
            two = jnp.where((lane >= TAIL) & (lane < 64), pltpu.roll(tile(STRIPS - 1, 3), TAIL - 8 * e, 1), two)
        return two

    def split(first, second):
        for t in range(TILES // 2):
            first[t * 8 : (t + 1) * 8, :] = packed(t)
            second[t * 8 : (t + 1) * 8, :] = packed(t + TILES // 2)

    core = lax.axis_index("core")
    pl.when(core == 0)(lambda: split(keep_ref, give_ref))
    pl.when(core == 1)(lambda: split(give_ref, keep_ref))


def add_kernel(a_ref, b_ref, out_ref):
    out_ref[...] = a_ref[...] + b_ref[...]


def sum_kernel(in_ref, out_ref):
    total = in_ref[0:24, :]
    for d in range(1, CHIPS // 2):
        total = total + in_ref[d * 24 : (d + 1) * 24, :]
    own = total[0:SLICE] + total[SLICE:24]
    twice = jnp.concatenate([own, own], axis=0)
    for d in range(CHIPS // 2):
        out_ref[d * 24 : (d + 1) * 24, :] = twice


def place_kernel(kept_ref, given_ref, out_hbm, out_ref, sent):
    lane = lane_index((8, LANES))
    copies = [
        pltpu.make_async_copy(out_ref.at[n * 88 : (n + 1) * 88], out_hbm.at[n * 88 : (n + 1) * 88], sent.at[n]) for n in range(5)
    ]

    def place(first, second):
        def tile(t):
            half, t = (first, t) if t < TILES // 2 else (second, t - TILES // 2)
            return half[t * 8 : (t + 1) * 8, :]

        for e in range(STRIPS):
            for chunk in range(3):
                out_ref[e * 8 : (e + 1) * 8, chunk * LANES : (chunk + 1) * LANES] = tile(e * 3 + chunk)
            if e < HALF:
                strip = tile(STRIPS * 3 + e)
            elif e < STRIPS - 1:
                strip = pltpu.roll(tile(STRIPS * 3 + e - HALF), 64, 1)
            else:
                strip = jnp.zeros((8, LANES), jnp.float32)
                for k in range(7):
                    piece = pltpu.roll(tile(STRIPS * 3 + k), (8 * k - TAIL) % LANES, 1)
                    strip = jnp.where((lane >= 8 * k) & (lane < 8 * k + 8), piece, strip)
            out_ref[e * 8 : (e + 1) * 8, 3 * LANES : 440] = strip[:, 0:TAIL]
            if e % 11 == 10:
                copies[e // 11].start()

    core = lax.axis_index("core")
    pl.when(core == 0)(lambda: place(kept_ref, given_ref))
    pl.when(core == 1)(lambda: place(given_ref, kept_ref))
    for copy in copies:
        copy.wait()


def exchange(x, axes, shape):
    return lax.all_to_all(x.reshape(shape), axes, 0, 0, tiled=True).reshape(x.shape)


def to_other_core(x):
    return lax.ppermute(x, "core", [(0, 1), (1, 0)])


def shards(final_amp, initial_amp, pair_final, pair_initial, map_final, map_initial, counts):
    vmem = pl.BlockSpec(memory_space=pltpu.VMEM)
    f32, bf16 = jnp.float32, jnp.bfloat16
    half = jax.ShapeDtypeStruct((CHIPS * SLICE, LANES), f32)

    def call(kernel, out_shape, n, scratch=()):
        several = isinstance(out_shape, list)
        return pl.pallas_call(
            kernel,
            out_shape=out_shape,
            in_specs=[vmem] * n,
            out_specs=[vmem] * len(out_shape) if several else vmem,
            scratch_shapes=list(scratch),
            compiler_params=PARAMS,
        )

    messages = pl.pallas_call(
        send_kernel,
        out_shape=jax.ShapeDtypeStruct((DEVICES * MESSAGE, LANES), bf16),
        in_specs=[pl.BlockSpec(memory_space=pltpu.SMEM)] + [pl.BlockSpec(memory_space=pltpu.HBM)] * 6,
        out_specs=vmem,
        scratch_shapes=[
            pltpu.VMEM((6, 440, LANES), bf16),
            pltpu.VMEM((1, 1, LANES), jnp.int32),
            pltpu.VMEM((1, 1, LANES), jnp.int32),
            pltpu.VMEM((1, 4, 440), jnp.int32),
            pltpu.VMEM((1, 2, 440), jnp.int32),
            pltpu.VMEM((8, 512), jnp.int32),
            pltpu.VMEM((DEVICES * MESSAGE, LANES), f32),
            pltpu.SemaphoreType.DMA((6,)),
        ],
        compiler_params=PARAMS,
    )(
        counts,
        *(
            pltpu.with_memory_space_constraint(x, pltpu.HBM)
            for x in (
                jnp.swapaxes(final_amp, 2, 3),
                jnp.swapaxes(initial_amp, 2, 3),
                pair_final,
                pair_initial,
                map_final,
                map_initial,
            )
        )
    )
    received = exchange(messages, ALL, (DEVICES, MESSAGE, LANES))
    keep, give = call(
        density_kernel,
        [half, half],
        1,
        [
            pltpu.VMEM((DEVICES * MESSAGE, LANES), f32),
            pltpu.VMEM((2 * LANES, LANES), f32),
            pltpu.VMEM((512, 512), bf16),
            pltpu.VMEM((512, 512), bf16),
            pltpu.VMEM((4 * 256, LANES), f32),
            pltpu.VMEM((512, 512), f32),
        ],
    )(received)
    share = call(add_kernel, half, 2)(keep, to_other_core(give))
    shares = exchange(share, ACROSS_CHIPS, (CHIPS, 3, 4, LANES))
    copies = call(sum_kernel, half, 1)(shares)
    slices = exchange(copies, ACROSS_CHIPS, (CHIPS, 3, 4, LANES))
    return pl.pallas_call(
        place_kernel,
        out_shape=jax.ShapeDtypeStruct((440, 440), f32),
        in_specs=[vmem] * 2,
        out_specs=pl.BlockSpec(memory_space=pltpu.HBM),
        scratch_shapes=[pltpu.VMEM((440, 440), f32), pltpu.SemaphoreType.DMA((5,))],
        compiler_params=PARAMS,
    )(slices, to_other_core(slices))


def solution(mesh):
    cores = Mesh(mesh.devices.reshape(4, 2, 2, 2, 4), ALL)
    row, col = ("x", "y_hi", "core"), ("y_lo", "z")
    placed = (
        P(row, col, None, None),
        P(col, row, None, None),
        P(row, col, None),
        P(row, col, None),
        P(row, col, None),
        P(col, row, None),
        P(row, col),
    )
    return jax.shard_map(shards, mesh=cores, in_specs=placed, out_specs=P(), check_vma=False)
```

```python
import jax
import jax.numpy as jnp
from jax import lax
from jax.experimental import pallas as pl
from jax.experimental.pallas import tpu as pltpu
from jax.sharding import Mesh
from jax.sharding import PartitionSpec as P

LANES = 128
DEVICES = 128
CHIPS = 64
FINAL_ROWS = 16
MESSAGE = 24
SLICE = 12
HALF_ORB = 220
FULL_TILES = 27
PACKED = 13
TAIL = 56
DEAD = 64
ALL = ("x", "y_hi", "core", "y_lo", "z")
ACROSS_CHIPS = ("x", "y_hi", "y_lo", "z")
PARAMS = pltpu.CompilerParams(vmem_limit_bytes=48 * 1024 * 1024)


def lane_index(shape):
    return lax.broadcasted_iota(jnp.int32, shape, len(shape) - 1)


def send_kernel(counts, finals, initials, pairs_final, pairs_initial, maps_final, maps_initial, out_ref, *scratch):
    blocks, pf, pi, mf, mi, maps, wide, arrived = scratch
    pairs = [
        (finals.at[0], blocks.at[0:4]),
        (initials.at[0], blocks.at[4:6]),
        (maps_final, mf),
        (maps_initial, mi),
        (pairs_final, pf),
        (pairs_initial, pi),
    ]
    copies = [pltpu.make_async_copy(there, here, arrived.at[n]) for n, (there, here) in enumerate(pairs)]
    for copy in copies:
        copy.start()
    maps[...] = jnp.full(maps.shape, -1, jnp.int32)
    for copy in copies:
        copy.wait()
    maps[0:4, 0:HALF_ORB] = mf[0, :, 0:HALF_ORB]
    maps[0:4, 256 : 256 + HALF_ORB] = mf[0, :, HALF_ORB:440]
    maps[4:6, 0:440] = mi[0]
    slot = lane_index((1, LANES))
    q = pf[0]
    s = pi[0]
    q_code = jnp.where(slot < counts[0, 0], (q & 3) * 8 + (q >> 2), DEAD).astype(jnp.float32)
    s_code = ((s & 1) * 16 + (s >> 1)).astype(jnp.float32)
    q_code = jnp.broadcast_to(q_code, (8, LANES))
    s_code = jnp.broadcast_to(s_code, (8, LANES))
    info = [pltpu.roll(code, (96 - 32 * m) % LANES, 1) for code in (q_code, s_code) for m in range(4)]
    last = lane_index((8, LANES)) >= 96
    for j in range(6):
        stored = lax.broadcasted_iota(jnp.int32, (440, 512), 0)
        pick = jnp.where(stored == maps[j : j + 1, :], 1.0, 0.0).astype(jnp.bfloat16)
        ordered = lax.dot_general(blocks[j], pick, (((0,), (0,)), ((), ())), preferred_element_type=jnp.float32)
        for chunk in range(4):
            part = ordered[:, chunk * LANES : (chunk + 1) * LANES]
            if j >= 4:
                wide[pl.ds(j * 4 + chunk, DEVICES, stride=MESSAGE), :] = part
                continue
            core, place = chunk // 2, chunk % 2
            for group in range(16):
                other = core ^ (group % 2)
                rows = part[group * 8 : (group + 1) * 8]
                if place == 1:
                    rows = jnp.where(last, info[j * 2 + other], rows)
                first = (group // 2 * 2 + core) * 8 * MESSAGE + j * 4 + other * 2 + place
                wide[pl.ds(first, 8, stride=MESSAGE), :] = rows
    out_ref[...] = wide[...].astype(jnp.bfloat16)


def widen_kernel(in_ref, wide, initial):
    wide[...] = in_ref[...].astype(jnp.float32)
    for j in range(2):
        for chunk in range(4):
            part = wide[pl.ds(FINAL_ROWS + j * 4 + chunk, DEVICES, stride=MESSAGE), :].astype(jnp.bfloat16)
            initial[j * LANES : (j + 1) * LANES, chunk * LANES : (chunk + 1) * LANES] = part


def times_kernel(wide, out_ref, pairs, final, met):
    quarter = lane_index((LANES, LANES)) // 32
    for k in range(2):
        codes = jnp.zeros((LANES, LANES), jnp.float32)
        for m in range(4):
            piece = wide[pl.ds(1 + 2 * m + 8 * k, DEVICES, stride=MESSAGE), :]
            codes = jnp.where(quarter == m, pltpu.roll(piece, (32 * m - 96) % LANES, 1), codes)
        pairs[k * LANES : (k + 1) * LANES, :] = codes

    for r in range(16):
        for chunk in range(4):
            part = [wide[pl.ds(r * 8 * MESSAGE + j * 4 + chunk, 8, stride=MESSAGE), :] for j in range(4)]
            final[r * 32 : (r + 1) * 32, chunk * LANES : (chunk + 1) * LANES] = jnp.concatenate(part, axis=0).astype(jnp.bfloat16)

    code = lax.broadcasted_iota(jnp.int32, (32, LANES), 0).astype(jnp.float32)

    def one_hot(slots):
        return jnp.where(code == slots, 1.0, 0.0).astype(jnp.bfloat16)

    for c in range(8):
        for g in range(4):
            cells = []
            for d in range(g * 32 + c, g * 32 + 32, 8):
                cells.append(
                    lax.dot_general(
                        one_hot(pairs[LANES + d : LANES + d + 1, :]),
                        one_hot(pairs[d : d + 1, :]),
                        (((1,), (1,)), ((), ())),
                        preferred_element_type=jnp.float32,
                    )
                )
            cells = jnp.concatenate(cells, axis=1)
            for j in range(2):
                met[pl.ds(g * 256 + j * LANES + c, 16, stride=8), :] = cells[j * 16 : (j + 1) * 16]

    times = jnp.concatenate([met[g * 256 : (g + 1) * 256, :].astype(jnp.bfloat16) for g in range(4)], axis=1)
    summed = jnp.dot(times, final[...], preferred_element_type=jnp.float32)
    high = summed.astype(jnp.bfloat16)
    low = (summed - high.astype(jnp.float32)).astype(jnp.bfloat16)
    for other in range(2):
        columns = slice(other * 256, (other + 1) * 256)
        out_ref[other * 512 : other * 512 + 256, :] = high[:, columns]
        out_ref[other * 512 + 256 : other * 512 + 512, :] = low[:, columns]


def density_kernel(summed_ref, own_ref, other_ref, out_ref, full):
    own, other = own_ref[...], other_ref[...]
    full[...] = lax.dot_general(
        summed_ref[...],
        jnp.concatenate([own, own, other, other], axis=0),
        (((0,), (0,)), ((), ())),
        preferred_element_type=jnp.float32,
    )
    lane = lane_index((8, LANES))
    upper = lax.broadcasted_iota(jnp.int32, (8, LANES), 0) < 4

    def tile(e, chunk):
        return full[e * 8 : (e + 1) * 8, chunk * LANES : (chunk + 1) * LANES]

    def put(t, value):
        out_ref[t * 8 : (t + 1) * 8, :] = value

    for e in range(FULL_TILES):
        for chunk in range(3):
            put(e * 3 + chunk, tile(e, chunk))
    for u in range(PACKED):
        two = jnp.where(lane < 64, tile(u, 3), pltpu.roll(tile(u + PACKED, 3), 64, 1))
        if u < 7:
            two = jnp.where((lane >= TAIL) & (lane < 64), pltpu.roll(tile(2 * PACKED, 3), TAIL - 8 * u, 1), two)
        put(FULL_TILES * 3 + u, two)
    for n in range(2):
        two = jnp.where(upper, tile(FULL_TILES, 2 * n), pltpu.roll(tile(FULL_TILES, 2 * n + 1), 4, 0))
        put(FULL_TILES * 3 + PACKED + n, two)


def sum_kernel(in_ref, out_ref):
    total = in_ref[0:24, :]
    for d in range(1, CHIPS // 2):
        total = total + in_ref[d * 24 : (d + 1) * 24, :]
    own = total[0:SLICE] + total[SLICE:24]
    twice = jnp.concatenate([own, own], axis=0)
    for d in range(CHIPS // 2):
        out_ref[d * 24 : (d + 1) * 24, :] = twice


def place_kernel(kept_ref, given_ref, out_hbm, out_ref, sent):
    lane = lane_index((8, LANES))
    upper = lax.broadcasted_iota(jnp.int32, (8, LANES), 0) < 4
    copies = [
        pltpu.make_async_copy(out_ref.at[n * 88 : (n + 1) * 88], out_hbm.at[n * 88 : (n + 1) * 88], sent.at[n]) for n in range(5)
    ]

    def tiles(half, e):
        def got(t):
            return half[t * 8 : (t + 1) * 8, :]

        packed = FULL_TILES * 3
        if e == FULL_TILES:
            rest = [got(packed + PACKED), got(packed + PACKED + 1)]
            return [rest[0], pltpu.roll(rest[0], 4, 0), rest[1], pltpu.roll(rest[1], 4, 0)]
        if e < PACKED:
            strip = got(packed + e)
        elif e < 2 * PACKED:
            strip = pltpu.roll(got(packed + e - PACKED), 64, 1)
        else:
            strip = jnp.zeros((8, LANES), jnp.float32)
            for k in range(7):
                piece = pltpu.roll(got(packed + k), (8 * k - TAIL) % LANES, 1)
                strip = jnp.where((lane >= 8 * k) & (lane < 8 * k + 8), piece, strip)
        return [got(e * 3), got(e * 3 + 1), got(e * 3 + 2), strip]

    def place(first, second):
        below = None
        for e in range(55):
            if e < FULL_TILES:
                row = tiles(first, e)
            else:
                above = tiles(first, e) if e == FULL_TILES else below
                below = [pltpu.roll(x, 4, 0) for x in tiles(second, e - FULL_TILES)]
                row = [jnp.where(upper, x, y) for x, y in zip(above, below)]
            for chunk in range(3):
                out_ref[e * 8 : (e + 1) * 8, chunk * LANES : (chunk + 1) * LANES] = row[chunk]
            out_ref[e * 8 : (e + 1) * 8, 3 * LANES : 440] = row[3][:, 0:TAIL]
            if e % 11 == 10:
                copies[e // 11].start()

    core = lax.axis_index("core")
    pl.when(core == 0)(lambda: place(kept_ref, given_ref))
    pl.when(core == 1)(lambda: place(given_ref, kept_ref))
    for copy in copies:
        copy.wait()


def exchange(x, axes, shape):
    return lax.all_to_all(x.reshape(shape), axes, 0, 0, tiled=True).reshape(x.shape)


def to_other_core(x):
    return lax.ppermute(x, "core", [(0, 1), (1, 0)])


def shards(final_amp, initial_amp, pair_final, pair_initial, map_final, map_initial, counts):
    vmem = pl.BlockSpec(memory_space=pltpu.VMEM)
    f32, bf16 = jnp.float32, jnp.bfloat16
    half = jax.ShapeDtypeStruct((CHIPS * SLICE, LANES), f32)

    def call(kernel, out_shape, n, scratch=(), cost=None):
        several = isinstance(out_shape, list)
        return pl.pallas_call(
            kernel,
            out_shape=out_shape,
            in_specs=[vmem] * n,
            out_specs=[vmem] * len(out_shape) if several else vmem,
            scratch_shapes=list(scratch),
            cost_estimate=cost,
            compiler_params=PARAMS,
        )

    messages = pl.pallas_call(
        send_kernel,
        out_shape=jax.ShapeDtypeStruct((DEVICES * MESSAGE, LANES), bf16),
        in_specs=[pl.BlockSpec(memory_space=pltpu.SMEM)] + [pl.BlockSpec(memory_space=pltpu.HBM)] * 6,
        out_specs=vmem,
        scratch_shapes=[
            pltpu.VMEM((6, 440, LANES), bf16),
            pltpu.VMEM((1, 1, LANES), jnp.int32),
            pltpu.VMEM((1, 1, LANES), jnp.int32),
            pltpu.VMEM((1, 4, 440), jnp.int32),
            pltpu.VMEM((1, 2, 440), jnp.int32),
            pltpu.VMEM((8, 512), jnp.int32),
            pltpu.VMEM((DEVICES * MESSAGE, LANES), f32),
            pltpu.SemaphoreType.DMA((6,)),
        ],
        compiler_params=PARAMS,
    )(
        counts,
        *(
            pltpu.with_memory_space_constraint(x, pltpu.HBM)
            for x in (
                jnp.swapaxes(final_amp, 2, 3),
                jnp.swapaxes(initial_amp, 2, 3),
                pair_final,
                pair_initial,
                map_final,
                map_initial,
            )
        )
    )
    received = exchange(messages, ALL, (DEVICES, MESSAGE, LANES))
    wide, own = call(
        widen_kernel,
        [jax.ShapeDtypeStruct((DEVICES * MESSAGE, LANES), f32), jax.ShapeDtypeStruct((256, 512), bf16)],
        1,
    )(received)
    other = to_other_core(own)
    summed = call(
        times_kernel,
        jax.ShapeDtypeStruct((1024, 256), bf16),
        1,
        [
            pltpu.VMEM((2 * LANES, LANES), f32),
            pltpu.VMEM((512, 512), bf16),
            pltpu.VMEM((4 * 256, LANES), f32),
        ],
        pl.CostEstimate(flops=10**9, bytes_accessed=8 * 10**6, transcendentals=0),
    )(wide)
    share = call(density_kernel, half, 3, [pltpu.VMEM((256, 512), f32)])(summed, own, other)
    shares = exchange(share, ACROSS_CHIPS, (CHIPS, 3, 4, LANES))
    copies = call(sum_kernel, half, 1)(shares)
    slices = exchange(copies, ACROSS_CHIPS, (CHIPS, 3, 4, LANES))
    return pl.pallas_call(
        place_kernel,
        out_shape=jax.ShapeDtypeStruct((440, 440), f32),
        in_specs=[vmem] * 2,
        out_specs=pl.BlockSpec(memory_space=pltpu.HBM),
        scratch_shapes=[pltpu.VMEM((440, 440), f32), pltpu.SemaphoreType.DMA((5,))],
        compiler_params=PARAMS,
    )(slices, to_other_core(slices))


def solution(mesh):
    cores = Mesh(mesh.devices.reshape(4, 2, 2, 2, 4), ALL)
    row, col = ("x", "y_hi", "core"), ("y_lo", "z")
    placed = (
        P(row, col, None, None),
        P(col, row, None, None),
        P(row, col, None),
        P(row, col, None),
        P(row, col, None),
        P(col, row, None),
        P(row, col),
    )
    return jax.shard_map(shards, mesh=cores, in_specs=placed, out_specs=P(), check_vma=False)
```

```python
import jax
import jax.numpy as jnp
from jax import lax
from jax.experimental import pallas as pl
from jax.experimental.pallas import tpu as pltpu
from jax.sharding import Mesh
from jax.sharding import PartitionSpec as P

LANES = 128
DEVICES = 128
CHIPS = 64
FINAL_ROWS = 16
MESSAGE = 24
SLICE = 12
HALF_ORB = 220
FULL_TILES = 27
PACKED = 13
TAIL = 56
DEAD = 64
ALL = ("x", "y_hi", "core", "y_lo", "z")
ACROSS_CHIPS = ("x", "y_hi", "y_lo", "z")
PARAMS = pltpu.CompilerParams(vmem_limit_bytes=48 * 1024 * 1024)


def lane_index(shape):
    return lax.broadcasted_iota(jnp.int32, shape, len(shape) - 1)


def send_kernel(counts, finals, initials, pairs_final, pairs_initial, maps_final, maps_initial, out_ref, *scratch):
    blocks, pf, pi, mf, mi, maps, wide, arrived = scratch
    pairs = [
        (finals.at[0], blocks.at[0:4]),
        (initials.at[0], blocks.at[4:6]),
        (maps_final, mf),
        (maps_initial, mi),
        (pairs_final, pf),
        (pairs_initial, pi),
    ]
    copies = [pltpu.make_async_copy(there, here, arrived.at[n]) for n, (there, here) in enumerate(pairs)]
    for copy in copies:
        copy.start()
    maps[...] = jnp.full(maps.shape, -1, jnp.int32)
    for copy in copies:
        copy.wait()
    maps[0:4, 0:HALF_ORB] = mf[0, :, 0:HALF_ORB]
    maps[0:4, 256 : 256 + HALF_ORB] = mf[0, :, HALF_ORB:440]
    maps[4:6, 0:440] = mi[0]
    slot = lane_index((1, LANES))
    q = pf[0]
    s = pi[0]
    q_code = jnp.where(slot < counts[0, 0], (q & 3) * 8 + (q >> 2), DEAD).astype(jnp.float32)
    s_code = ((s & 1) * 16 + (s >> 1)).astype(jnp.float32)
    q_code = jnp.broadcast_to(q_code, (8, LANES))
    s_code = jnp.broadcast_to(s_code, (8, LANES))
    info = [pltpu.roll(code, (96 - 32 * m) % LANES, 1) for code in (q_code, s_code) for m in range(4)]
    last = lane_index((8, LANES)) >= 96
    for j in range(6):
        stored = lax.broadcasted_iota(jnp.int32, (440, 512), 0)
        pick = jnp.where(stored == maps[j : j + 1, :], 1.0, 0.0).astype(jnp.bfloat16)
        ordered = lax.dot_general(blocks[j], pick, (((0,), (0,)), ((), ())), preferred_element_type=jnp.float32)
        for chunk in range(4):
            part = ordered[:, chunk * LANES : (chunk + 1) * LANES]
            if j >= 4:
                wide[pl.ds(j * 4 + chunk, DEVICES, stride=MESSAGE), :] = part
                continue
            core, place = chunk // 2, chunk % 2
            for group in range(16):
                other = core ^ (group % 2)
                rows = part[group * 8 : (group + 1) * 8]
                if place == 1:
                    rows = jnp.where(last, info[j * 2 + other], rows)
                first = (group // 2 * 2 + core) * 8 * MESSAGE + j * 4 + other * 2 + place
                wide[pl.ds(first, 8, stride=MESSAGE), :] = rows
    out_ref[...] = wide[...].astype(jnp.bfloat16)


def widen_kernel(in_ref, wide, initial):
    wide[...] = in_ref[...].astype(jnp.float32)
    for j in range(2):
        for chunk in range(4):
            part = wide[pl.ds(FINAL_ROWS + j * 4 + chunk, DEVICES, stride=MESSAGE), :].astype(jnp.bfloat16)
            initial[j * LANES : (j + 1) * LANES, chunk * LANES : (chunk + 1) * LANES] = part


def times_kernel(wide, out_ref, pairs, final, met):
    quarter = lane_index((LANES, LANES)) // 32
    for k in range(2):
        codes = jnp.zeros((LANES, LANES), jnp.float32)
        for m in range(4):
            piece = wide[pl.ds(1 + 2 * m + 8 * k, DEVICES, stride=MESSAGE), :]
            codes = jnp.where(quarter == m, pltpu.roll(piece, (32 * m - 96) % LANES, 1), codes)
        pairs[k * LANES : (k + 1) * LANES, :] = codes

    for r in range(16):
        for chunk in range(4):
            part = [wide[pl.ds(r * 8 * MESSAGE + j * 4 + chunk, 8, stride=MESSAGE), :] for j in range(4)]
            final[r * 32 : (r + 1) * 32, chunk * LANES : (chunk + 1) * LANES] = jnp.concatenate(part, axis=0).astype(jnp.bfloat16)

    code = lax.broadcasted_iota(jnp.int32, (32, LANES), 0).astype(jnp.float32)

    def one_hot(slots):
        return jnp.where(code == slots, 1.0, 0.0).astype(jnp.bfloat16)

    for c in range(8):
        for g in range(4):
            cells = []
            for d in range(g * 32 + c, g * 32 + 32, 8):
                cells.append(
                    lax.dot_general(
                        one_hot(pairs[LANES + d : LANES + d + 1, :]),
                        one_hot(pairs[d : d + 1, :]),
                        (((1,), (1,)), ((), ())),
                        preferred_element_type=jnp.float32,
                    )
                )
            cells = jnp.concatenate(cells, axis=1)
            for j in range(2):
                met[pl.ds(g * 256 + j * LANES + c, 16, stride=8), :] = cells[j * 16 : (j + 1) * 16]

    times = jnp.concatenate([met[g * 256 : (g + 1) * 256, :].astype(jnp.bfloat16) for g in range(4)], axis=1)
    summed = jnp.dot(times, final[...], preferred_element_type=jnp.float32)
    high = summed.astype(jnp.bfloat16)
    low = (summed - high.astype(jnp.float32)).astype(jnp.bfloat16)
    for other in range(2):
        columns = slice(other * 256, (other + 1) * 256)
        out_ref[other * 512 : other * 512 + 256, :] = high[:, columns]
        out_ref[other * 512 + 256 : other * 512 + 512, :] = low[:, columns]


def density_kernel(summed_ref, own_ref, other_ref, out_ref, full):
    own, other = own_ref[...], other_ref[...]
    full[...] = lax.dot_general(
        summed_ref[...],
        jnp.concatenate([own, own, other, other], axis=0),
        (((0,), (0,)), ((), ())),
        preferred_element_type=jnp.float32,
    )
    lane = lane_index((8, LANES))
    upper = lax.broadcasted_iota(jnp.int32, (8, LANES), 0) < 4

    def tile(e, chunk):
        return full[e * 8 : (e + 1) * 8, chunk * LANES : (chunk + 1) * LANES]

    def put(t, value):
        out_ref[t * 8 : (t + 1) * 8, :] = value

    for e in range(FULL_TILES):
        for chunk in range(3):
            put(e * 3 + chunk, tile(e, chunk))
    for u in range(PACKED):
        two = jnp.where(lane < 64, tile(u, 3), pltpu.roll(tile(u + PACKED, 3), 64, 1))
        if u < 7:
            two = jnp.where((lane >= TAIL) & (lane < 64), pltpu.roll(tile(2 * PACKED, 3), TAIL - 8 * u, 1), two)
        put(FULL_TILES * 3 + u, two)
    for n in range(2):
        two = jnp.where(upper, tile(FULL_TILES, 2 * n), pltpu.roll(tile(FULL_TILES, 2 * n + 1), 4, 0))
        put(FULL_TILES * 3 + PACKED + n, two)


def sum_kernel(in_ref, out_ref):
    total = in_ref[0:24, :]
    for d in range(1, CHIPS // 2):
        total = total + in_ref[d * 24 : (d + 1) * 24, :]
    own = total[0:SLICE] + total[SLICE:24]
    twice = jnp.concatenate([own, own], axis=0)
    for d in range(CHIPS // 2):
        out_ref[d * 24 : (d + 1) * 24, :] = twice


def density_rows(first, second, start, stop):
    lane = lane_index((8, LANES))
    upper = lax.broadcasted_iota(jnp.int32, (8, LANES), 0) < 4
    packed = FULL_TILES * 3

    def tiles(half, e):
        def got(t):
            return half[t * 8 : (t + 1) * 8, :]

        if e == FULL_TILES:
            rest = [got(packed + PACKED), got(packed + PACKED + 1)]
            return [rest[0], pltpu.roll(rest[0], 4, 0), rest[1], pltpu.roll(rest[1], 4, 0)]
        if e < PACKED:
            strip = got(packed + e)
        elif e < 2 * PACKED:
            strip = pltpu.roll(got(packed + e - PACKED), 64, 1)
        else:
            strip = jnp.zeros((8, LANES), jnp.float32)
            for k in range(7):
                piece = pltpu.roll(got(packed + k), (8 * k - TAIL) % LANES, 1)
                strip = jnp.where((lane >= 8 * k) & (lane < 8 * k + 8), piece, strip)
        return [got(e * 3), got(e * 3 + 1), got(e * 3 + 2), strip]

    def turned(e):
        return [pltpu.roll(x, 4, 0) for x in tiles(second, e)]

    below = None
    for e in range(start, stop):
        if e < FULL_TILES:
            yield tiles(first, e)
            continue
        above = tiles(first, e) if e == FULL_TILES else turned(e - FULL_TILES - 1) if below is None else below
        below = turned(e - FULL_TILES)
        yield [jnp.where(upper, x, y) for x, y in zip(above, below)]


def put_rows(first, second, start, stop, chunk, out_hbm, out_ref, sent):
    copies = []
    for n, row in enumerate(density_rows(first, second, start, stop)):
        for c in range(3):
            out_ref[n * 8 : (n + 1) * 8, c * LANES : (c + 1) * LANES] = row[c]
        out_ref[n * 8 : (n + 1) * 8, 3 * LANES : 440] = row[3][:, 0:TAIL]
        if n % chunk == chunk - 1:
            here = slice((n - chunk + 1) * 8, (n + 1) * 8)
            there = slice((start + n - chunk + 1) * 8, (start + n + 1) * 8)
            copies.append(pltpu.make_async_copy(out_ref.at[here], out_hbm.at[there], sent.at[n // chunk]))
            copies[-1].start()
    for copy in copies:
        copy.wait()


def place_own_kernel(kept_ref, out_hbm, out_ref, sent):
    core = lax.axis_index("core")
    pl.when(core == 0)(lambda: put_rows(kept_ref, None, 0, FULL_TILES, 9, out_hbm, out_ref, sent))
    pl.when(core == 1)(lambda: put_rows(None, kept_ref, FULL_TILES + 1, 55, 9, out_hbm, out_ref, sent))


def place_other_kernel(kept_ref, given_ref, placed, out_hbm, out_ref, sent):
    del placed
    core = lax.axis_index("core")
    pl.when(core == 0)(lambda: put_rows(kept_ref, given_ref, FULL_TILES, 55, 7, out_hbm, out_ref, sent))
    pl.when(core == 1)(lambda: put_rows(given_ref, kept_ref, 0, FULL_TILES + 1, 7, out_hbm, out_ref, sent))


def exchange(x, axes, shape):
    return lax.all_to_all(x.reshape(shape), axes, 0, 0, tiled=True).reshape(x.shape)


def to_other_core(x):
    return lax.ppermute(x, "core", [(0, 1), (1, 0)])


def shards(final_amp, initial_amp, pair_final, pair_initial, map_final, map_initial, counts):
    vmem = pl.BlockSpec(memory_space=pltpu.VMEM)
    f32, bf16 = jnp.float32, jnp.bfloat16
    half = jax.ShapeDtypeStruct((CHIPS * SLICE, LANES), f32)

    def call(kernel, out_shape, n, scratch=(), cost=None):
        several = isinstance(out_shape, list)
        return pl.pallas_call(
            kernel,
            out_shape=out_shape,
            in_specs=[vmem] * n,
            out_specs=[vmem] * len(out_shape) if several else vmem,
            scratch_shapes=list(scratch),
            cost_estimate=cost,
            compiler_params=PARAMS,
        )

    messages = pl.pallas_call(
        send_kernel,
        out_shape=jax.ShapeDtypeStruct((DEVICES * MESSAGE, LANES), bf16),
        in_specs=[pl.BlockSpec(memory_space=pltpu.SMEM)] + [pl.BlockSpec(memory_space=pltpu.HBM)] * 6,
        out_specs=vmem,
        scratch_shapes=[
            pltpu.VMEM((6, 440, LANES), bf16),
            pltpu.VMEM((1, 1, LANES), jnp.int32),
            pltpu.VMEM((1, 1, LANES), jnp.int32),
            pltpu.VMEM((1, 4, 440), jnp.int32),
            pltpu.VMEM((1, 2, 440), jnp.int32),
            pltpu.VMEM((8, 512), jnp.int32),
            pltpu.VMEM((DEVICES * MESSAGE, LANES), f32),
            pltpu.SemaphoreType.DMA((6,)),
        ],
        compiler_params=PARAMS,
    )(
        counts,
        *(
            pltpu.with_memory_space_constraint(x, pltpu.HBM)
            for x in (
                jnp.swapaxes(final_amp, 2, 3),
                jnp.swapaxes(initial_amp, 2, 3),
                pair_final,
                pair_initial,
                map_final,
                map_initial,
            )
        )
    )
    received = exchange(messages, ALL, (DEVICES, MESSAGE, LANES))
    wide, own = call(
        widen_kernel,
        [jax.ShapeDtypeStruct((DEVICES * MESSAGE, LANES), f32), jax.ShapeDtypeStruct((256, 512), bf16)],
        1,
    )(received)
    other = to_other_core(own)
    summed = call(
        times_kernel,
        jax.ShapeDtypeStruct((1024, 256), bf16),
        1,
        [
            pltpu.VMEM((2 * LANES, LANES), f32),
            pltpu.VMEM((512, 512), bf16),
            pltpu.VMEM((4 * 256, LANES), f32),
        ],
        pl.CostEstimate(flops=10**9, bytes_accessed=8 * 10**6, transcendentals=0),
    )(wide)
    share = call(density_kernel, half, 3, [pltpu.VMEM((256, 512), f32)])(summed, own, other)
    shares = exchange(share, ACROSS_CHIPS, (CHIPS, 3, 4, LANES))
    copies = call(sum_kernel, half, 1)(shares)
    slices = exchange(copies, ACROSS_CHIPS, (CHIPS, 3, 4, LANES))
    hbm = pl.BlockSpec(memory_space=pltpu.HBM)
    other_slices = to_other_core(slices)
    density = jax.ShapeDtypeStruct((440, 440), f32)
    placed = pl.pallas_call(
        place_own_kernel,
        out_shape=density,
        in_specs=[vmem],
        out_specs=hbm,
        scratch_shapes=[pltpu.VMEM((FULL_TILES * 8, 440), f32), pltpu.SemaphoreType.DMA((3,))],
        cost_estimate=pl.CostEstimate(flops=10**6, bytes_accessed=4 * 10**6, transcendentals=0),
        compiler_params=PARAMS,
    )(slices)
    return pl.pallas_call(
        place_other_kernel,
        out_shape=density,
        in_specs=[vmem, vmem, hbm],
        out_specs=hbm,
        scratch_shapes=[pltpu.VMEM(((FULL_TILES + 1) * 8, 440), f32), pltpu.SemaphoreType.DMA((4,))],
        input_output_aliases={2: 0},
        compiler_params=PARAMS,
    )(slices, other_slices, placed)


def solution(mesh):
    cores = Mesh(mesh.devices.reshape(4, 2, 2, 2, 4), ALL)
    row, col = ("x", "y_hi", "core"), ("y_lo", "z")
    placed = (
        P(row, col, None, None),
        P(col, row, None, None),
        P(row, col, None),
        P(row, col, None),
        P(row, col, None),
        P(col, row, None),
        P(row, col),
    )
    return jax.shard_map(shards, mesh=cores, in_specs=placed, out_specs=P(), check_vma=False)
```

```python
import jax
import jax.numpy as jnp
from jax import lax
from jax.experimental import pallas as pl
from jax.experimental.pallas import tpu as pltpu
from jax.sharding import Mesh
from jax.sharding import PartitionSpec as P

LANES = 128
DEVICES = 128
CHIPS = 64
FINAL_ROWS = 16
MESSAGE = 24
SLICE = 12
HALF_ORB = 220
FULL_TILES = 27
PACKED = 13
TAIL = 56
DEAD = 64
ALL = ("x", "y_hi", "core", "y_lo", "z")
ACROSS_CHIPS = ("x", "y_hi", "y_lo", "z")
PARAMS = pltpu.CompilerParams(vmem_limit_bytes=48 * 1024 * 1024)


def lane_index(shape):
    return lax.broadcasted_iota(jnp.int32, shape, len(shape) - 1)


def send_kernel(counts, finals, initials, pairs_final, pairs_initial, maps_final, maps_initial, out_ref, *scratch):
    blocks, pf, pi, mf, mi, maps, wide, arrived = scratch
    pairs = [
        (finals.at[0], blocks.at[0:4]),
        (initials.at[0], blocks.at[4:6]),
        (maps_final, mf),
        (maps_initial, mi),
        (pairs_final, pf),
        (pairs_initial, pi),
    ]
    copies = [pltpu.make_async_copy(there, here, arrived.at[n]) for n, (there, here) in enumerate(pairs)]
    for copy in copies:
        copy.start()
    maps[...] = jnp.full(maps.shape, -1, jnp.int32)
    for copy in copies:
        copy.wait()
    maps[0:4, 0:HALF_ORB] = mf[0, :, 0:HALF_ORB]
    maps[0:4, 256 : 256 + HALF_ORB] = mf[0, :, HALF_ORB:440]
    maps[4:6, 0:440] = mi[0]
    slot = lane_index((1, LANES))
    q = pf[0]
    s = pi[0]
    q_code = jnp.where(slot < counts[0, 0], (q & 3) * 8 + (q >> 2), DEAD).astype(jnp.float32)
    s_code = ((s & 1) * 16 + (s >> 1)).astype(jnp.float32)
    q_code = jnp.broadcast_to(q_code, (8, LANES))
    s_code = jnp.broadcast_to(s_code, (8, LANES))
    info = [pltpu.roll(code, (96 - 32 * m) % LANES, 1) for code in (q_code, s_code) for m in range(4)]
    last = lane_index((8, LANES)) >= 96
    for j in range(6):
        stored = lax.broadcasted_iota(jnp.int32, (440, 512), 0)
        pick = jnp.where(stored == maps[j : j + 1, :], 1.0, 0.0).astype(jnp.bfloat16)
        ordered = lax.dot_general(blocks[j], pick, (((0,), (0,)), ((), ())), preferred_element_type=jnp.float32)
        for chunk in range(4):
            part = ordered[:, chunk * LANES : (chunk + 1) * LANES]
            if j >= 4:
                wide[pl.ds(j * 4 + chunk, DEVICES, stride=MESSAGE), :] = part
                continue
            core, place = chunk // 2, chunk % 2
            for group in range(16):
                other = core ^ (group % 2)
                rows = part[group * 8 : (group + 1) * 8]
                if place == 1:
                    rows = jnp.where(last, info[j * 2 + other], rows)
                first = (group // 2 * 2 + core) * 8 * MESSAGE + j * 4 + other * 2 + place
                wide[pl.ds(first, 8, stride=MESSAGE), :] = rows
    out_ref[...] = wide[...].astype(jnp.bfloat16)


def widen_kernel(in_ref, wide, initial):
    wide[...] = in_ref[...].astype(jnp.float32)
    for j in range(2):
        for chunk in range(4):
            part = wide[pl.ds(FINAL_ROWS + j * 4 + chunk, DEVICES, stride=MESSAGE), :].astype(jnp.bfloat16)
            initial[j * LANES : (j + 1) * LANES, chunk * LANES : (chunk + 1) * LANES] = part


def times_kernel(wide, own_ref, part_ref, out_ref, pairs, final, met):
    quarter = lane_index((LANES, LANES)) // 32
    for k in range(2):
        codes = jnp.zeros((LANES, LANES), jnp.float32)
        for m in range(4):
            piece = wide[pl.ds(1 + 2 * m + 8 * k, DEVICES, stride=MESSAGE), :]
            codes = jnp.where(quarter == m, pltpu.roll(piece, (32 * m - 96) % LANES, 1), codes)
        pairs[k * LANES : (k + 1) * LANES, :] = codes

    for r in range(16):
        for chunk in range(4):
            part = [wide[pl.ds(r * 8 * MESSAGE + j * 4 + chunk, 8, stride=MESSAGE), :] for j in range(4)]
            final[r * 32 : (r + 1) * 32, chunk * LANES : (chunk + 1) * LANES] = jnp.concatenate(part, axis=0).astype(jnp.bfloat16)

    code = lax.broadcasted_iota(jnp.int32, (32, LANES), 0).astype(jnp.float32)

    def one_hot(slots):
        return jnp.where(code == slots, 1.0, 0.0).astype(jnp.bfloat16)

    for c in range(8):
        for g in range(4):
            cells = []
            for d in range(g * 32 + c, g * 32 + 32, 8):
                cells.append(
                    lax.dot_general(
                        one_hot(pairs[LANES + d : LANES + d + 1, :]),
                        one_hot(pairs[d : d + 1, :]),
                        (((1,), (1,)), ((), ())),
                        preferred_element_type=jnp.float32,
                    )
                )
            cells = jnp.concatenate(cells, axis=1)
            for j in range(2):
                met[pl.ds(g * 256 + j * LANES + c, 16, stride=8), :] = cells[j * 16 : (j + 1) * 16]

    times = jnp.concatenate([met[g * 256 : (g + 1) * 256, :].astype(jnp.bfloat16) for g in range(4)], axis=1)
    summed = jnp.dot(times, final[...], preferred_element_type=jnp.float32)
    high = summed.astype(jnp.bfloat16)
    low = (summed - high.astype(jnp.float32)).astype(jnp.bfloat16)
    own = own_ref[...]
    part_ref[...] = lax.dot_general(
        jnp.concatenate([high[:, 0:256], low[:, 0:256]], axis=0),
        jnp.concatenate([own, own], axis=0),
        (((0,), (0,)), ((), ())),
        preferred_element_type=jnp.float32,
    )
    out_ref[0:256, :] = high[:, 256:512]
    out_ref[256:512, :] = low[:, 256:512]


def density_kernel(part_ref, summed_ref, other_ref, out_ref, full):
    other = other_ref[...]
    full[...] = part_ref[...] + lax.dot_general(
        summed_ref[...],
        jnp.concatenate([other, other], axis=0),
        (((0,), (0,)), ((), ())),
        preferred_element_type=jnp.float32,
    )
    lane = lane_index((8, LANES))
    upper = lax.broadcasted_iota(jnp.int32, (8, LANES), 0) < 4

    def tile(e, chunk):
        return full[e * 8 : (e + 1) * 8, chunk * LANES : (chunk + 1) * LANES]

    def put(t, value):
        out_ref[t * 8 : (t + 1) * 8, :] = value

    for e in range(FULL_TILES):
        for chunk in range(3):
            put(e * 3 + chunk, tile(e, chunk))
    for u in range(PACKED):
        two = jnp.where(lane < 64, tile(u, 3), pltpu.roll(tile(u + PACKED, 3), 64, 1))
        if u < 7:
            two = jnp.where((lane >= TAIL) & (lane < 64), pltpu.roll(tile(2 * PACKED, 3), TAIL - 8 * u, 1), two)
        put(FULL_TILES * 3 + u, two)
    for n in range(2):
        two = jnp.where(upper, tile(FULL_TILES, 2 * n), pltpu.roll(tile(FULL_TILES, 2 * n + 1), 4, 0))
        put(FULL_TILES * 3 + PACKED + n, two)


def sum_kernel(in_ref, out_ref):
    total = in_ref[0:24, :]
    for d in range(1, CHIPS // 2):
        total = total + in_ref[d * 24 : (d + 1) * 24, :]
    own = total[0:SLICE] + total[SLICE:24]
    twice = jnp.concatenate([own, own], axis=0)
    for d in range(CHIPS // 2):
        out_ref[d * 24 : (d + 1) * 24, :] = twice


def density_rows(first, second, start, stop):
    lane = lane_index((8, LANES))
    upper = lax.broadcasted_iota(jnp.int32, (8, LANES), 0) < 4
    packed = FULL_TILES * 3

    def tiles(half, e):
        def got(t):
            return half[t * 8 : (t + 1) * 8, :]

        if e == FULL_TILES:
            rest = [got(packed + PACKED), got(packed + PACKED + 1)]
            return [rest[0], pltpu.roll(rest[0], 4, 0), rest[1], pltpu.roll(rest[1], 4, 0)]
        if e < PACKED:
            strip = got(packed + e)
        elif e < 2 * PACKED:
            strip = pltpu.roll(got(packed + e - PACKED), 64, 1)
        else:
            strip = jnp.zeros((8, LANES), jnp.float32)
            for k in range(7):
                piece = pltpu.roll(got(packed + k), (8 * k - TAIL) % LANES, 1)
                strip = jnp.where((lane >= 8 * k) & (lane < 8 * k + 8), piece, strip)
        return [got(e * 3), got(e * 3 + 1), got(e * 3 + 2), strip]

    def turned(e):
        return [pltpu.roll(x, 4, 0) for x in tiles(second, e)]

    below = None
    for e in range(start, stop):
        if e < FULL_TILES:
            yield tiles(first, e)
            continue
        above = tiles(first, e) if e == FULL_TILES else turned(e - FULL_TILES - 1) if below is None else below
        below = turned(e - FULL_TILES)
        yield [jnp.where(upper, x, y) for x, y in zip(above, below)]


def put_rows(first, second, start, stop, chunk, out_hbm, out_ref, sent):
    copies = []
    for n, row in enumerate(density_rows(first, second, start, stop)):
        for c in range(3):
            out_ref[n * 8 : (n + 1) * 8, c * LANES : (c + 1) * LANES] = row[c]
        out_ref[n * 8 : (n + 1) * 8, 3 * LANES : 440] = row[3][:, 0:TAIL]
        if n % chunk == chunk - 1:
            here = slice((n - chunk + 1) * 8, (n + 1) * 8)
            there = slice((start + n - chunk + 1) * 8, (start + n + 1) * 8)
            copies.append(pltpu.make_async_copy(out_ref.at[here], out_hbm.at[there], sent.at[n // chunk]))
            copies[-1].start()
    for copy in copies:
        copy.wait()


def place_own_kernel(kept_ref, out_hbm, out_ref, sent):
    core = lax.axis_index("core")
    pl.when(core == 0)(lambda: put_rows(kept_ref, None, 0, FULL_TILES, 9, out_hbm, out_ref, sent))
    pl.when(core == 1)(lambda: put_rows(None, kept_ref, FULL_TILES + 1, 55, 9, out_hbm, out_ref, sent))


def place_other_kernel(kept_ref, given_ref, placed, out_hbm, out_ref, sent):
    del placed
    core = lax.axis_index("core")
    pl.when(core == 0)(lambda: put_rows(kept_ref, given_ref, FULL_TILES, 55, 7, out_hbm, out_ref, sent))
    pl.when(core == 1)(lambda: put_rows(given_ref, kept_ref, 0, FULL_TILES + 1, 7, out_hbm, out_ref, sent))


def exchange(x, axes, shape):
    return lax.all_to_all(x.reshape(shape), axes, 0, 0, tiled=True).reshape(x.shape)


def to_other_core(x):
    return lax.ppermute(x, "core", [(0, 1), (1, 0)])


def shards(final_amp, initial_amp, pair_final, pair_initial, map_final, map_initial, counts):
    vmem = pl.BlockSpec(memory_space=pltpu.VMEM)
    f32, bf16 = jnp.float32, jnp.bfloat16
    half = jax.ShapeDtypeStruct((CHIPS * SLICE, LANES), f32)

    def call(kernel, out_shape, n, scratch=(), cost=None):
        several = isinstance(out_shape, list)
        return pl.pallas_call(
            kernel,
            out_shape=out_shape,
            in_specs=[vmem] * n,
            out_specs=[vmem] * len(out_shape) if several else vmem,
            scratch_shapes=list(scratch),
            cost_estimate=cost,
            compiler_params=PARAMS,
        )

    messages = pl.pallas_call(
        send_kernel,
        out_shape=jax.ShapeDtypeStruct((DEVICES * MESSAGE, LANES), bf16),
        in_specs=[pl.BlockSpec(memory_space=pltpu.SMEM)] + [pl.BlockSpec(memory_space=pltpu.HBM)] * 6,
        out_specs=vmem,
        scratch_shapes=[
            pltpu.VMEM((6, 440, LANES), bf16),
            pltpu.VMEM((1, 1, LANES), jnp.int32),
            pltpu.VMEM((1, 1, LANES), jnp.int32),
            pltpu.VMEM((1, 4, 440), jnp.int32),
            pltpu.VMEM((1, 2, 440), jnp.int32),
            pltpu.VMEM((8, 512), jnp.int32),
            pltpu.VMEM((DEVICES * MESSAGE, LANES), f32),
            pltpu.SemaphoreType.DMA((6,)),
        ],
        compiler_params=PARAMS,
    )(
        counts,
        *(
            pltpu.with_memory_space_constraint(x, pltpu.HBM)
            for x in (
                jnp.swapaxes(final_amp, 2, 3),
                jnp.swapaxes(initial_amp, 2, 3),
                pair_final,
                pair_initial,
                map_final,
                map_initial,
            )
        )
    )
    received = exchange(messages, ALL, (DEVICES, MESSAGE, LANES))
    wide, own = call(
        widen_kernel,
        [jax.ShapeDtypeStruct((DEVICES * MESSAGE, LANES), f32), jax.ShapeDtypeStruct((256, 512), bf16)],
        1,
    )(received)
    other = to_other_core(own)
    part, summed = call(
        times_kernel,
        [jax.ShapeDtypeStruct((256, 512), f32), jax.ShapeDtypeStruct((512, 256), bf16)],
        2,
        [
            pltpu.VMEM((2 * LANES, LANES), f32),
            pltpu.VMEM((512, 512), bf16),
            pltpu.VMEM((4 * 256, LANES), f32),
        ],
        pl.CostEstimate(flops=10**9, bytes_accessed=8 * 10**6, transcendentals=0),
    )(wide, own)
    share = call(density_kernel, half, 3, [pltpu.VMEM((256, 512), f32)])(part, summed, other)
    shares = exchange(share, ACROSS_CHIPS, (CHIPS, 3, 4, LANES))
    copies = call(sum_kernel, half, 1)(shares)
    slices = exchange(copies, ACROSS_CHIPS, (CHIPS, 3, 4, LANES))
    hbm = pl.BlockSpec(memory_space=pltpu.HBM)
    other_slices = to_other_core(slices)
    density = jax.ShapeDtypeStruct((440, 440), f32)
    placed = pl.pallas_call(
        place_own_kernel,
        out_shape=density,
        in_specs=[vmem],
        out_specs=hbm,
        scratch_shapes=[pltpu.VMEM((FULL_TILES * 8, 440), f32), pltpu.SemaphoreType.DMA((3,))],
        cost_estimate=pl.CostEstimate(flops=10**6, bytes_accessed=4 * 10**6, transcendentals=0),
        compiler_params=PARAMS,
    )(slices)
    return pl.pallas_call(
        place_other_kernel,
        out_shape=density,
        in_specs=[vmem, vmem, hbm],
        out_specs=hbm,
        scratch_shapes=[pltpu.VMEM(((FULL_TILES + 1) * 8, 440), f32), pltpu.SemaphoreType.DMA((4,))],
        input_output_aliases={2: 0},
        compiler_params=PARAMS,
    )(slices, other_slices, placed)


def solution(mesh):
    cores = Mesh(mesh.devices.reshape(4, 2, 2, 2, 4), ALL)
    row, col = ("x", "y_hi", "core"), ("y_lo", "z")
    placed = (
        P(row, col, None, None),
        P(col, row, None, None),
        P(row, col, None),
        P(row, col, None),
        P(row, col, None),
        P(col, row, None),
        P(row, col),
    )
    return jax.shard_map(shards, mesh=cores, in_specs=placed, out_specs=P(), check_vma=False)
```

```python
import jax
import jax.numpy as jnp
from jax import lax
from jax.experimental import pallas as pl
from jax.experimental.pallas import tpu as pltpu
from jax.sharding import Mesh
from jax.sharding import PartitionSpec as P

LANES = 128
DEVICES = 128
CHIPS = 64
FINAL_ROWS = 16
MESSAGE = 24
SLICE = 12
HALF_ORB = 220
FULL_TILES = 27
PACKED = 13
TAIL = 56
DEAD = 64
ALL = ("x", "y_hi", "core", "y_lo", "z")
ACROSS_CHIPS = ("x", "y_hi", "y_lo", "z")
PARAMS = pltpu.CompilerParams(vmem_limit_bytes=48 * 1024 * 1024)


def lane_index(shape):
    return lax.broadcasted_iota(jnp.int32, shape, len(shape) - 1)


def send_kernel(counts, finals, initials, pairs_final, pairs_initial, maps_final, maps_initial, out_ref, *scratch):
    blocks, pf, pi, mf, mi, maps, wide, arrived = scratch
    pairs = [
        (finals.at[0], blocks.at[0:4]),
        (initials.at[0], blocks.at[4:6]),
        (maps_final, mf),
        (maps_initial, mi),
        (pairs_final, pf),
        (pairs_initial, pi),
    ]
    copies = [pltpu.make_async_copy(there, here, arrived.at[n]) for n, (there, here) in enumerate(pairs)]
    for copy in copies:
        copy.start()
    maps[...] = jnp.full(maps.shape, -1, jnp.int32)
    for copy in copies:
        copy.wait()
    maps[0:4, 0:HALF_ORB] = mf[0, :, 0:HALF_ORB]
    maps[0:4, 256 : 256 + HALF_ORB] = mf[0, :, HALF_ORB:440]
    maps[4:6, 0:440] = mi[0]
    slot = lane_index((1, LANES))
    q = pf[0]
    s = pi[0]
    q_code = jnp.where(slot < counts[0, 0], (q & 3) * 8 + (q >> 2), DEAD).astype(jnp.float32)
    s_code = ((s & 1) * 16 + (s >> 1)).astype(jnp.float32)
    q_code = jnp.broadcast_to(q_code, (8, LANES))
    s_code = jnp.broadcast_to(s_code, (8, LANES))
    info = [pltpu.roll(code, (96 - 32 * m) % LANES, 1) for code in (q_code, s_code) for m in range(4)]
    last = lane_index((8, LANES)) >= 96
    stored = lax.broadcasted_iota(jnp.int32, (440, 512), 0).astype(jnp.int16)
    one, zero = jnp.ones((440, 512), jnp.bfloat16), jnp.zeros((440, 512), jnp.bfloat16)
    for j in range(6):
        wanted = jnp.broadcast_to(maps[j : j + 1, :], (440, 512)).astype(jnp.int16)
        pick = jnp.where(stored == wanted, one, zero)
        ordered = lax.dot_general(blocks[j], pick, (((0,), (0,)), ((), ())), preferred_element_type=jnp.float32)
        for chunk in range(4):
            part = ordered[:, chunk * LANES : (chunk + 1) * LANES]
            if j >= 4:
                wide[pl.ds(j * 4 + chunk, DEVICES, stride=MESSAGE), :] = part
                continue
            core, place = chunk // 2, chunk % 2
            for group in range(16):
                other = core ^ (group % 2)
                rows = part[group * 8 : (group + 1) * 8]
                if place == 1:
                    rows = jnp.where(last, info[j * 2 + other], rows)
                first = (group // 2 * 2 + core) * 8 * MESSAGE + j * 4 + other * 2 + place
                wide[pl.ds(first, 8, stride=MESSAGE), :] = rows
    out_ref[...] = wide[...].astype(jnp.bfloat16)


def initial_kernel(in_ref, initial, wide):
    for d in range(0, DEVICES, 2):
        both = in_ref[d * MESSAGE : (d + 2) * MESSAGE, :].astype(jnp.float32)
        wide[d * 8 : (d + 1) * 8, :] = both[FINAL_ROWS:MESSAGE]
        wide[(d + 1) * 8 : (d + 2) * 8, :] = both[MESSAGE + FINAL_ROWS :]
    for j in range(2):
        for chunk in range(4):
            part = wide[pl.ds(j * 4 + chunk, DEVICES, stride=8), :].astype(jnp.bfloat16)
            initial[j * LANES : (j + 1) * LANES, chunk * LANES : (chunk + 1) * LANES] = part


def times_kernel(in_ref, out_ref, wide, pairs, final, met):
    wide[...] = in_ref[...].astype(jnp.float32)
    quarter = lane_index((LANES, LANES)) // 32
    for k in range(2):
        codes = jnp.zeros((LANES, LANES), jnp.float32)
        for m in range(4):
            piece = wide[pl.ds(1 + 2 * m + 8 * k, DEVICES, stride=MESSAGE), :]
            codes = jnp.where(quarter == m, pltpu.roll(piece, (32 * m - 96) % LANES, 1), codes)
        pairs[k * LANES : (k + 1) * LANES, :] = codes

    for r in range(16):
        for chunk in range(4):
            part = [wide[pl.ds(r * 8 * MESSAGE + j * 4 + chunk, 8, stride=MESSAGE), :] for j in range(4)]
            final[r * 32 : (r + 1) * 32, chunk * LANES : (chunk + 1) * LANES] = jnp.concatenate(part, axis=0).astype(jnp.bfloat16)

    code = lax.broadcasted_iota(jnp.int32, (32, LANES), 0).astype(jnp.float32)

    def one_hot(slots):
        return jnp.where(code == slots, 1.0, 0.0).astype(jnp.bfloat16)

    for c in range(8):
        for g in range(4):
            cells = []
            for d in range(g * 32 + c, g * 32 + 32, 8):
                cells.append(
                    lax.dot_general(
                        one_hot(pairs[LANES + d : LANES + d + 1, :]),
                        one_hot(pairs[d : d + 1, :]),
                        (((1,), (1,)), ((), ())),
                        preferred_element_type=jnp.float32,
                    )
                )
            cells = jnp.concatenate(cells, axis=1)
            for j in range(2):
                met[pl.ds(g * 256 + j * LANES + c, 16, stride=8), :] = cells[j * 16 : (j + 1) * 16]

    times = jnp.concatenate([met[g * 256 : (g + 1) * 256, :].astype(jnp.bfloat16) for g in range(4)], axis=1)
    summed = jnp.dot(times, final[...], preferred_element_type=jnp.float32)
    high = summed.astype(jnp.bfloat16)
    low = (summed - high.astype(jnp.float32)).astype(jnp.bfloat16)
    for other in range(2):
        columns = slice(other * 256, (other + 1) * 256)
        out_ref[other * 512 : other * 512 + 256, :] = high[:, columns]
        out_ref[other * 512 + 256 : other * 512 + 512, :] = low[:, columns]


def density_kernel(summed_ref, own_ref, other_ref, out_ref, full):
    own, other = own_ref[...], other_ref[...]
    full[...] = lax.dot_general(
        summed_ref[...],
        jnp.concatenate([own, own, other, other], axis=0),
        (((0,), (0,)), ((), ())),
        preferred_element_type=jnp.float32,
    )
    lane = lane_index((8, LANES))
    upper = lax.broadcasted_iota(jnp.int32, (8, LANES), 0) < 4

    def tile(e, chunk):
        return full[e * 8 : (e + 1) * 8, chunk * LANES : (chunk + 1) * LANES]

    def put(t, value):
        out_ref[t * 8 : (t + 1) * 8, :] = value

    for e in range(FULL_TILES):
        for chunk in range(3):
            put(e * 3 + chunk, tile(e, chunk))
    for u in range(PACKED):
        two = jnp.where(lane < 64, tile(u, 3), pltpu.roll(tile(u + PACKED, 3), 64, 1))
        if u < 7:
            two = jnp.where((lane >= TAIL) & (lane < 64), pltpu.roll(tile(2 * PACKED, 3), TAIL - 8 * u, 1), two)
        put(FULL_TILES * 3 + u, two)
    for n in range(2):
        two = jnp.where(upper, tile(FULL_TILES, 2 * n), pltpu.roll(tile(FULL_TILES, 2 * n + 1), 4, 0))
        put(FULL_TILES * 3 + PACKED + n, two)


def sum_kernel(in_ref, out_ref):
    total = in_ref[0:24, :]
    for d in range(1, CHIPS // 2):
        total = total + in_ref[d * 24 : (d + 1) * 24, :]
    own = total[0:SLICE] + total[SLICE:24]
    twice = jnp.concatenate([own, own], axis=0)
    for d in range(CHIPS // 2):
        out_ref[d * 24 : (d + 1) * 24, :] = twice


def density_rows(first, second, start, stop):
    lane = lane_index((8, LANES))
    upper = lax.broadcasted_iota(jnp.int32, (8, LANES), 0) < 4
    packed = FULL_TILES * 3

    def tiles(half, e):
        def got(t):
            return half[t * 8 : (t + 1) * 8, :]

        if e == FULL_TILES:
            rest = [got(packed + PACKED), got(packed + PACKED + 1)]
            return [rest[0], pltpu.roll(rest[0], 4, 0), rest[1], pltpu.roll(rest[1], 4, 0)]
        if e < PACKED:
            strip = got(packed + e)
        elif e < 2 * PACKED:
            strip = pltpu.roll(got(packed + e - PACKED), 64, 1)
        else:
            strip = jnp.zeros((8, LANES), jnp.float32)
            for k in range(7):
                piece = pltpu.roll(got(packed + k), (8 * k - TAIL) % LANES, 1)
                strip = jnp.where((lane >= 8 * k) & (lane < 8 * k + 8), piece, strip)
        return [got(e * 3), got(e * 3 + 1), got(e * 3 + 2), strip]

    def turned(e):
        return [pltpu.roll(x, 4, 0) for x in tiles(second, e)]

    below = None
    for e in range(start, stop):
        if e < FULL_TILES:
            yield tiles(first, e)
            continue
        above = tiles(first, e) if e == FULL_TILES else turned(e - FULL_TILES - 1) if below is None else below
        below = turned(e - FULL_TILES)
        yield [jnp.where(upper, x, y) for x, y in zip(above, below)]


def put_rows(first, second, start, stop, chunk, out_hbm, out_ref, sent):
    copies = []
    for n, row in enumerate(density_rows(first, second, start, stop)):
        for c in range(3):
            out_ref[n * 8 : (n + 1) * 8, c * LANES : (c + 1) * LANES] = row[c]
        out_ref[n * 8 : (n + 1) * 8, 3 * LANES : 440] = row[3][:, 0:TAIL]
        if n % chunk == chunk - 1:
            here = slice((n - chunk + 1) * 8, (n + 1) * 8)
            there = slice((start + n - chunk + 1) * 8, (start + n + 1) * 8)
            copies.append(pltpu.make_async_copy(out_ref.at[here], out_hbm.at[there], sent.at[n // chunk]))
            copies[-1].start()
    for copy in copies:
        copy.wait()


def place_own_kernel(kept_ref, out_hbm, out_ref, sent):
    core = lax.axis_index("core")
    pl.when(core == 0)(lambda: put_rows(kept_ref, None, 0, FULL_TILES, 9, out_hbm, out_ref, sent))
    pl.when(core == 1)(lambda: put_rows(None, kept_ref, FULL_TILES + 1, 55, 9, out_hbm, out_ref, sent))


def place_other_kernel(kept_ref, given_ref, placed, out_hbm, out_ref, sent):
    del placed
    core = lax.axis_index("core")
    pl.when(core == 0)(lambda: put_rows(kept_ref, given_ref, FULL_TILES, 55, 7, out_hbm, out_ref, sent))
    pl.when(core == 1)(lambda: put_rows(given_ref, kept_ref, 0, FULL_TILES + 1, 7, out_hbm, out_ref, sent))


def exchange(x, axes, shape):
    return lax.all_to_all(x.reshape(shape), axes, 0, 0, tiled=True).reshape(x.shape)


def to_other_core(x):
    return lax.ppermute(x, "core", [(0, 1), (1, 0)])


def shards(final_amp, initial_amp, pair_final, pair_initial, map_final, map_initial, counts):
    vmem = pl.BlockSpec(memory_space=pltpu.VMEM)
    f32, bf16 = jnp.float32, jnp.bfloat16
    half = jax.ShapeDtypeStruct((CHIPS * SLICE, LANES), f32)

    def call(kernel, out_shape, n, scratch=(), cost=None):
        several = isinstance(out_shape, list)
        return pl.pallas_call(
            kernel,
            out_shape=out_shape,
            in_specs=[vmem] * n,
            out_specs=[vmem] * len(out_shape) if several else vmem,
            scratch_shapes=list(scratch),
            cost_estimate=cost,
            compiler_params=PARAMS,
        )

    messages = pl.pallas_call(
        send_kernel,
        out_shape=jax.ShapeDtypeStruct((DEVICES * MESSAGE, LANES), bf16),
        in_specs=[pl.BlockSpec(memory_space=pltpu.SMEM)] + [pl.BlockSpec(memory_space=pltpu.HBM)] * 6,
        out_specs=vmem,
        scratch_shapes=[
            pltpu.VMEM((6, 440, LANES), bf16),
            pltpu.VMEM((1, 1, LANES), jnp.int32),
            pltpu.VMEM((1, 1, LANES), jnp.int32),
            pltpu.VMEM((1, 4, 440), jnp.int32),
            pltpu.VMEM((1, 2, 440), jnp.int32),
            pltpu.VMEM((8, 512), jnp.int32),
            pltpu.VMEM((DEVICES * MESSAGE, LANES), f32),
            pltpu.SemaphoreType.DMA((6,)),
        ],
        compiler_params=PARAMS,
    )(
        counts,
        *(
            pltpu.with_memory_space_constraint(x, pltpu.HBM)
            for x in (
                jnp.swapaxes(final_amp, 2, 3),
                jnp.swapaxes(initial_amp, 2, 3),
                pair_final,
                pair_initial,
                map_final,
                map_initial,
            )
        )
    )
    received = exchange(messages, ALL, (DEVICES, MESSAGE, LANES))
    own = call(
        initial_kernel, jax.ShapeDtypeStruct((256, 512), bf16), 1, [pltpu.VMEM((DEVICES * 8, LANES), f32)]
    )(received)
    other = to_other_core(own)
    summed = call(
        times_kernel,
        jax.ShapeDtypeStruct((1024, 256), bf16),
        1,
        [
            pltpu.VMEM((DEVICES * MESSAGE, LANES), f32),
            pltpu.VMEM((2 * LANES, LANES), f32),
            pltpu.VMEM((512, 512), bf16),
            pltpu.VMEM((4 * 256, LANES), f32),
        ],
        pl.CostEstimate(flops=10**9, bytes_accessed=8 * 10**6, transcendentals=0),
    )(received)
    share = call(density_kernel, half, 3, [pltpu.VMEM((256, 512), f32)])(summed, own, other)
    shares = exchange(share, ACROSS_CHIPS, (CHIPS, 3, 4, LANES))
    copies = call(sum_kernel, half, 1)(shares)
    slices = exchange(copies, ACROSS_CHIPS, (CHIPS, 3, 4, LANES))
    hbm = pl.BlockSpec(memory_space=pltpu.HBM)
    other_slices = to_other_core(slices)
    density = jax.ShapeDtypeStruct((440, 440), f32)
    placed = pl.pallas_call(
        place_own_kernel,
        out_shape=density,
        in_specs=[vmem],
        out_specs=hbm,
        scratch_shapes=[pltpu.VMEM((FULL_TILES * 8, 440), f32), pltpu.SemaphoreType.DMA((3,))],
        cost_estimate=pl.CostEstimate(flops=10**6, bytes_accessed=4 * 10**6, transcendentals=0),
        compiler_params=PARAMS,
    )(slices)
    return pl.pallas_call(
        place_other_kernel,
        out_shape=density,
        in_specs=[vmem, vmem, hbm],
        out_specs=hbm,
        scratch_shapes=[pltpu.VMEM(((FULL_TILES + 1) * 8, 440), f32), pltpu.SemaphoreType.DMA((4,))],
        input_output_aliases={2: 0},
        compiler_params=PARAMS,
    )(slices, other_slices, placed)


def solution(mesh):
    cores = Mesh(mesh.devices.reshape(4, 2, 2, 2, 4), ALL)
    row, col = ("x", "y_hi", "core"), ("y_lo", "z")
    placed = (
        P(row, col, None, None),
        P(col, row, None, None),
        P(row, col, None),
        P(row, col, None),
        P(row, col, None),
        P(col, row, None),
        P(row, col),
    )
    return jax.shard_map(shards, mesh=cores, in_specs=placed, out_specs=P(), check_vma=False)
```

```python
import jax
import jax.numpy as jnp
from jax import lax
from jax.experimental import pallas as pl
from jax.experimental.pallas import tpu as pltpu
from jax.sharding import Mesh
from jax.sharding import PartitionSpec as P

LANES = 128
DEVICES = 128
CHIPS = 64
FINAL_ROWS = 16
MESSAGE = 24
SLICE = 12
HALF_ORB = 220
FULL_TILES = 27
PACKED = 13
TAIL = 56
DEAD = 64
ALL = ("x", "y_hi", "core", "y_lo", "z")
ACROSS_CHIPS = ("x", "y_hi", "y_lo", "z")
PARAMS = pltpu.CompilerParams(vmem_limit_bytes=48 * 1024 * 1024)


def lane_index(shape):
    return lax.broadcasted_iota(jnp.int32, shape, len(shape) - 1)


def send_kernel(counts, finals, initials, pairs_final, pairs_initial, maps_final, maps_initial, out_ref, *scratch):
    blocks, pf, pi, mf, mi, maps, wide, arrived = scratch
    pairs = [
        (finals.at[0], blocks.at[0:4]),
        (initials.at[0], blocks.at[4:6]),
        (maps_final, mf),
        (maps_initial, mi),
        (pairs_final, pf),
        (pairs_initial, pi),
    ]
    copies = [pltpu.make_async_copy(there, here, arrived.at[n]) for n, (there, here) in enumerate(pairs)]
    for copy in copies:
        copy.start()
    maps[...] = jnp.full(maps.shape, -1, jnp.int32)
    for copy in copies:
        copy.wait()
    maps[0:4, 0:HALF_ORB] = mf[0, :, 0:HALF_ORB]
    maps[0:4, 256 : 256 + HALF_ORB] = mf[0, :, HALF_ORB:440]
    maps[4:6, 0:440] = mi[0]
    slot = lane_index((1, LANES))
    q = pf[0]
    s = pi[0]
    q_code = jnp.where(slot < counts[0, 0], (q & 3) * 8 + (q >> 2), DEAD).astype(jnp.float32)
    s_code = ((s & 1) * 16 + (s >> 1)).astype(jnp.float32)
    q_code = jnp.broadcast_to(q_code, (8, LANES))
    s_code = jnp.broadcast_to(s_code, (8, LANES))
    info = [pltpu.roll(code, (96 - 32 * m) % LANES, 1) for code in (q_code, s_code) for m in range(4)]
    last = lane_index((8, LANES)) >= 96
    stored = lax.broadcasted_iota(jnp.int32, (440, 512), 0).astype(jnp.int16)
    one, zero = jnp.ones((440, 512), jnp.bfloat16), jnp.zeros((440, 512), jnp.bfloat16)
    for j in range(6):
        wanted = jnp.broadcast_to(maps[j : j + 1, :], (440, 512)).astype(jnp.int16)
        pick = jnp.where(stored == wanted, one, zero)
        ordered = lax.dot_general(blocks[j], pick, (((0,), (0,)), ((), ())), preferred_element_type=jnp.float32)
        for chunk in range(4):
            part = ordered[:, chunk * LANES : (chunk + 1) * LANES]
            if j >= 4:
                wide[pl.ds(j * 4 + chunk, DEVICES, stride=MESSAGE), :] = part
                continue
            core, place = chunk // 2, chunk % 2
            for group in range(16):
                other = core ^ (group % 2)
                rows = part[group * 8 : (group + 1) * 8]
                if place == 1:
                    rows = jnp.where(last, info[j * 2 + other], rows)
                first = (group // 2 * 2 + core) * 8 * MESSAGE + j * 4 + other * 2 + place
                wide[pl.ds(first, 8, stride=MESSAGE), :] = rows
    out_ref[...] = wide[...].astype(jnp.bfloat16)


def initial_kernel(in_ref, initial, wide):
    for d in range(0, DEVICES, 2):
        both = in_ref[d * MESSAGE : (d + 2) * MESSAGE, :].astype(jnp.float32)
        wide[d * 8 : (d + 1) * 8, :] = both[FINAL_ROWS:MESSAGE]
        wide[(d + 1) * 8 : (d + 2) * 8, :] = both[MESSAGE + FINAL_ROWS :]
    for j in range(2):
        for chunk in range(4):
            part = wide[pl.ds(j * 4 + chunk, DEVICES, stride=8), :].astype(jnp.bfloat16)
            initial[j * LANES : (j + 1) * LANES, chunk * LANES : (chunk + 1) * LANES] = part


def times_kernel(in_ref, out_ref, wide, pairs, final, met):
    wide[...] = in_ref[...].astype(jnp.float32)
    quarter = lane_index((LANES, LANES)) // 32
    for k in range(2):
        codes = jnp.zeros((LANES, LANES), jnp.float32)
        for m in range(4):
            piece = wide[pl.ds(1 + 2 * m + 8 * k, DEVICES, stride=MESSAGE), :]
            codes = jnp.where(quarter == m, pltpu.roll(piece, (32 * m - 96) % LANES, 1), codes)
        pairs[k * LANES : (k + 1) * LANES, :] = codes

    for r in range(16):
        for chunk in range(4):
            part = [wide[pl.ds(r * 8 * MESSAGE + j * 4 + chunk, 8, stride=MESSAGE), :] for j in range(4)]
            final[r * 32 : (r + 1) * 32, chunk * LANES : (chunk + 1) * LANES] = jnp.concatenate(part, axis=0).astype(jnp.bfloat16)

    code = lax.broadcasted_iota(jnp.int32, (32, LANES), 0).astype(jnp.float32)

    def one_hot(slots):
        return jnp.where(code == slots, 1.0, 0.0).astype(jnp.bfloat16)

    for c in range(8):
        for g in range(4):
            cells = []
            for d in range(g * 32 + c, g * 32 + 32, 8):
                cells.append(
                    lax.dot_general(
                        one_hot(pairs[LANES + d : LANES + d + 1, :]),
                        one_hot(pairs[d : d + 1, :]),
                        (((1,), (1,)), ((), ())),
                        preferred_element_type=jnp.float32,
                    )
                )
            cells = jnp.concatenate(cells, axis=1)
            for j in range(2):
                met[pl.ds(g * 256 + j * LANES + c, 16, stride=8), :] = cells[j * 16 : (j + 1) * 16]

    times = jnp.concatenate([met[g * 256 : (g + 1) * 256, :].astype(jnp.bfloat16) for g in range(4)], axis=1)
    summed = jnp.dot(times, final[...], preferred_element_type=jnp.float32)
    high = summed.astype(jnp.bfloat16)
    low = (summed - high.astype(jnp.float32)).astype(jnp.bfloat16)
    for other in range(2):
        columns = slice(other * 256, (other + 1) * 256)
        out_ref[other * 512 : other * 512 + 256, :] = high[:, columns]
        out_ref[other * 512 + 256 : other * 512 + 512, :] = low[:, columns]


def density_kernel(summed_ref, own_ref, other_ref, out_ref, full):
    own, other = own_ref[...], other_ref[...]
    full[...] = lax.dot_general(
        summed_ref[...],
        jnp.concatenate([own, own, other, other], axis=0),
        (((0,), (0,)), ((), ())),
        preferred_element_type=jnp.float32,
    )
    lane = lane_index((8, LANES))
    upper = lax.broadcasted_iota(jnp.int32, (8, LANES), 0) < 4

    def tile(e, chunk):
        return full[e * 8 : (e + 1) * 8, chunk * LANES : (chunk + 1) * LANES]

    def put(t, value):
        out_ref[t * 8 : (t + 1) * 8, :] = value

    for e in range(FULL_TILES):
        for chunk in range(3):
            put(e * 3 + chunk, tile(e, chunk))
    for u in range(PACKED):
        two = jnp.where(lane < 64, tile(u, 3), pltpu.roll(tile(u + PACKED, 3), 64, 1))
        if u < 7:
            two = jnp.where((lane >= TAIL) & (lane < 64), pltpu.roll(tile(2 * PACKED, 3), TAIL - 8 * u, 1), two)
        put(FULL_TILES * 3 + u, two)
    for n in range(2):
        two = jnp.where(upper, tile(FULL_TILES, 2 * n), pltpu.roll(tile(FULL_TILES, 2 * n + 1), 4, 0))
        put(FULL_TILES * 3 + PACKED + n, two)


def sum_kernel(in_ref, out_ref):
    total = in_ref[0:24, :]
    for d in range(1, CHIPS // 2):
        total = total + in_ref[d * 24 : (d + 1) * 24, :]
    own = total[0:SLICE] + total[SLICE:24]
    twice = jnp.concatenate([own, own], axis=0)
    for d in range(CHIPS // 2):
        out_ref[d * 24 : (d + 1) * 24, :] = twice


def density_rows(first, second, start, stop):
    lane = lane_index((8, LANES))
    upper = lax.broadcasted_iota(jnp.int32, (8, LANES), 0) < 4
    packed = FULL_TILES * 3

    def tiles(half, e):
        def got(t):
            return half[t * 8 : (t + 1) * 8, :]

        if e == FULL_TILES:
            rest = [got(packed + PACKED), got(packed + PACKED + 1)]
            return [rest[0], pltpu.roll(rest[0], 4, 0), rest[1], pltpu.roll(rest[1], 4, 0)]
        if e < PACKED:
            strip = got(packed + e)
        elif e < 2 * PACKED:
            strip = pltpu.roll(got(packed + e - PACKED), 64, 1)
        else:
            strip = jnp.zeros((8, LANES), jnp.float32)
            for k in range(7):
                piece = pltpu.roll(got(packed + k), (8 * k - TAIL) % LANES, 1)
                strip = jnp.where((lane >= 8 * k) & (lane < 8 * k + 8), piece, strip)
        return [got(e * 3), got(e * 3 + 1), got(e * 3 + 2), strip]

    def turned(e):
        return [pltpu.roll(x, 4, 0) for x in tiles(second, e)]

    below = None
    for e in range(start, stop):
        if e < FULL_TILES:
            yield tiles(first, e)
            continue
        above = tiles(first, e) if e == FULL_TILES else turned(e - FULL_TILES - 1) if below is None else below
        below = turned(e - FULL_TILES)
        yield [jnp.where(upper, x, y) for x, y in zip(above, below)]


def put_rows(first, second, start, stop, chunk, out_hbm, out_ref, sent):
    copies = []
    for n, row in enumerate(density_rows(first, second, start, stop)):
        for c in range(3):
            out_ref[n * 8 : (n + 1) * 8, c * LANES : (c + 1) * LANES] = row[c]
        out_ref[n * 8 : (n + 1) * 8, 3 * LANES : 440] = row[3][:, 0:TAIL]
        if n % chunk == chunk - 1:
            here = slice((n - chunk + 1) * 8, (n + 1) * 8)
            there = slice((start + n - chunk + 1) * 8, (start + n + 1) * 8)
            copies.append(pltpu.make_async_copy(out_ref.at[here], out_hbm.at[there], sent.at[n // chunk]))
            copies[-1].start()
    for copy in copies:
        copy.wait()


def place_kernel(kept_ref, given_ref, out_hbm, out_ref, sent):
    core = lax.axis_index("core")
    pl.when(core == 0)(lambda: put_rows(kept_ref, given_ref, 0, 55, 11, out_hbm, out_ref, sent))
    pl.when(core == 1)(lambda: put_rows(given_ref, kept_ref, 0, 55, 11, out_hbm, out_ref, sent))


def exchange(x, axes, shape):
    return lax.all_to_all(x.reshape(shape), axes, 0, 0, tiled=True).reshape(x.shape)


def to_other_core(x):
    return lax.ppermute(x, "core", [(0, 1), (1, 0)])


def shards(final_amp, initial_amp, pair_final, pair_initial, map_final, map_initial, counts):
    vmem = pl.BlockSpec(memory_space=pltpu.VMEM)
    f32, bf16 = jnp.float32, jnp.bfloat16
    half = jax.ShapeDtypeStruct((CHIPS * SLICE, LANES), f32)

    def call(kernel, out_shape, n, scratch=(), cost=None):
        several = isinstance(out_shape, list)
        return pl.pallas_call(
            kernel,
            out_shape=out_shape,
            in_specs=[vmem] * n,
            out_specs=[vmem] * len(out_shape) if several else vmem,
            scratch_shapes=list(scratch),
            cost_estimate=cost,
            compiler_params=PARAMS,
        )

    messages = pl.pallas_call(
        send_kernel,
        out_shape=jax.ShapeDtypeStruct((DEVICES * MESSAGE, LANES), bf16),
        in_specs=[pl.BlockSpec(memory_space=pltpu.SMEM)] + [pl.BlockSpec(memory_space=pltpu.HBM)] * 6,
        out_specs=vmem,
        scratch_shapes=[
            pltpu.VMEM((6, 440, LANES), bf16),
            pltpu.VMEM((1, 1, LANES), jnp.int32),
            pltpu.VMEM((1, 1, LANES), jnp.int32),
            pltpu.VMEM((1, 4, 440), jnp.int32),
            pltpu.VMEM((1, 2, 440), jnp.int32),
            pltpu.VMEM((8, 512), jnp.int32),
            pltpu.VMEM((DEVICES * MESSAGE, LANES), f32),
            pltpu.SemaphoreType.DMA((6,)),
        ],
        compiler_params=PARAMS,
    )(
        counts,
        *(
            pltpu.with_memory_space_constraint(x, pltpu.HBM)
            for x in (
                jnp.swapaxes(final_amp, 2, 3),
                jnp.swapaxes(initial_amp, 2, 3),
                pair_final,
                pair_initial,
                map_final,
                map_initial,
            )
        )
    )
    received = exchange(messages, ALL, (DEVICES, MESSAGE, LANES))
    own = call(
        initial_kernel, jax.ShapeDtypeStruct((256, 512), bf16), 1, [pltpu.VMEM((DEVICES * 8, LANES), f32)]
    )(received)
    other = to_other_core(own)
    summed = call(
        times_kernel,
        jax.ShapeDtypeStruct((1024, 256), bf16),
        1,
        [
            pltpu.VMEM((DEVICES * MESSAGE, LANES), f32),
            pltpu.VMEM((2 * LANES, LANES), f32),
            pltpu.VMEM((512, 512), bf16),
            pltpu.VMEM((4 * 256, LANES), f32),
        ],
        pl.CostEstimate(flops=10**9, bytes_accessed=8 * 10**6, transcendentals=0),
    )(received)
    share = call(density_kernel, half, 3, [pltpu.VMEM((256, 512), f32)])(summed, own, other)
    shares = exchange(share, ACROSS_CHIPS, (CHIPS, 3, 4, LANES))
    copies = call(sum_kernel, half, 1)(shares)
    slices = exchange(copies, ACROSS_CHIPS, (CHIPS, 3, 4, LANES))
    hbm = pl.BlockSpec(memory_space=pltpu.HBM)
    return pl.pallas_call(
        place_kernel,
        out_shape=jax.ShapeDtypeStruct((440, 440), f32),
        in_specs=[vmem, vmem],
        out_specs=hbm,
        scratch_shapes=[pltpu.VMEM((440, 440), f32), pltpu.SemaphoreType.DMA((5,))],
        compiler_params=PARAMS,
    )(slices, to_other_core(slices))


def solution(mesh):
    cores = Mesh(mesh.devices.reshape(4, 2, 2, 2, 4), ALL)
    row, col = ("x", "y_hi", "core"), ("y_lo", "z")
    placed = (
        P(row, col, None, None),
        P(col, row, None, None),
        P(row, col, None),
        P(row, col, None),
        P(row, col, None),
        P(col, row, None),
        P(row, col),
    )
    return jax.shard_map(shards, mesh=cores, in_specs=placed, out_specs=P(), check_vma=False)
```

```python
import jax
import jax.numpy as jnp
from jax import lax
from jax.experimental import pallas as pl
from jax.experimental.pallas import tpu as pltpu
from jax.sharding import Mesh
from jax.sharding import PartitionSpec as P

LANES = 128
DEVICES = 128
CHIPS = 64
FINAL_ROWS = 16
MESSAGE = 24
SLICE = 12
HALF_ORB = 220
FULL_TILES = 27
PACKED = 13
TAIL = 56
DEAD = 64
ALL = ("x", "y_hi", "core", "y_lo", "z")
ACROSS_CHIPS = ("x", "y_hi", "y_lo", "z")
PARAMS = pltpu.CompilerParams(vmem_limit_bytes=48 * 1024 * 1024)


def lane_index(shape):
    return lax.broadcasted_iota(jnp.int32, shape, len(shape) - 1)


def send_kernel(counts, finals, initials, pairs_final, pairs_initial, maps_final, maps_initial, out_ref, *scratch):
    blocks, pf, pi, mf, mi, maps, wide, arrived = scratch
    pairs = [
        (finals.at[0], blocks.at[0:4]),
        (initials.at[0], blocks.at[4:6]),
        (maps_final, mf),
        (maps_initial, mi),
        (pairs_final, pf),
        (pairs_initial, pi),
    ]
    copies = [pltpu.make_async_copy(there, here, arrived.at[n]) for n, (there, here) in enumerate(pairs)]
    for copy in copies:
        copy.start()
    maps[...] = jnp.full(maps.shape, -1, jnp.int32)
    for copy in copies:
        copy.wait()
    maps[0:4, 0:HALF_ORB] = mf[0, :, 0:HALF_ORB]
    maps[0:4, 256 : 256 + HALF_ORB] = mf[0, :, HALF_ORB:440]
    maps[4:6, 0:440] = mi[0]
    slot = lane_index((1, LANES))
    q = pf[0]
    s = pi[0]
    q_code = jnp.where(slot < counts[0, 0], (q & 3) * 8 + (q >> 2), DEAD).astype(jnp.float32)
    s_code = ((s & 1) * 16 + (s >> 1)).astype(jnp.float32)
    q_code = jnp.broadcast_to(q_code, (8, LANES))
    s_code = jnp.broadcast_to(s_code, (8, LANES))
    info = [pltpu.roll(code, (96 - 32 * m) % LANES, 1) for code in (q_code, s_code) for m in range(4)]
    last = lane_index((8, LANES)) >= 96
    stored = lax.broadcasted_iota(jnp.int32, (440, 512), 0).astype(jnp.int16)
    one, zero = jnp.ones((440, 512), jnp.bfloat16), jnp.zeros((440, 512), jnp.bfloat16)
    for j in range(6):
        wanted = jnp.broadcast_to(maps[j : j + 1, :], (440, 512)).astype(jnp.int16)
        pick = jnp.where(stored == wanted, one, zero)
        ordered = lax.dot_general(blocks[j], pick, (((0,), (0,)), ((), ())), preferred_element_type=jnp.float32)
        for chunk in range(4):
            part = ordered[:, chunk * LANES : (chunk + 1) * LANES]
            if j >= 4:
                wide[pl.ds(j * 4 + chunk, DEVICES, stride=MESSAGE), :] = part
                continue
            core, place = chunk // 2, chunk % 2
            for group in range(16):
                other = core ^ (group % 2)
                rows = part[group * 8 : (group + 1) * 8]
                if place == 1:
                    rows = jnp.where(last, info[j * 2 + other], rows)
                first = (group // 2 * 2 + core) * 8 * MESSAGE + j * 4 + other * 2 + place
                wide[pl.ds(first, 8, stride=MESSAGE), :] = rows
    out_ref[...] = wide[...].astype(jnp.bfloat16)


def initial_kernel(in_ref, initial, wide):
    for d in range(0, DEVICES, 2):
        both = in_ref[d * MESSAGE : (d + 2) * MESSAGE, :].astype(jnp.float32)
        wide[d * 8 : (d + 1) * 8, :] = both[FINAL_ROWS:MESSAGE]
        wide[(d + 1) * 8 : (d + 2) * 8, :] = both[MESSAGE + FINAL_ROWS :]
    for j in range(2):
        for chunk in range(4):
            part = wide[pl.ds(j * 4 + chunk, DEVICES, stride=8), :].astype(jnp.bfloat16)
            initial[j * LANES : (j + 1) * LANES, chunk * LANES : (chunk + 1) * LANES] = part


def times_kernel(in_ref, own_ref, part_ref, out_ref, wide, pairs, final, met):
    wide[...] = in_ref[...].astype(jnp.float32)
    quarter = lane_index((LANES, LANES)) // 32
    for k in range(2):
        codes = jnp.zeros((LANES, LANES), jnp.float32)
        for m in range(4):
            piece = wide[pl.ds(1 + 2 * m + 8 * k, DEVICES, stride=MESSAGE), :]
            codes = jnp.where(quarter == m, pltpu.roll(piece, (32 * m - 96) % LANES, 1), codes)
        pairs[k * LANES : (k + 1) * LANES, :] = codes

    for r in range(16):
        for chunk in range(4):
            part = [wide[pl.ds(r * 8 * MESSAGE + j * 4 + chunk, 8, stride=MESSAGE), :] for j in range(4)]
            final[r * 32 : (r + 1) * 32, chunk * LANES : (chunk + 1) * LANES] = jnp.concatenate(part, axis=0).astype(jnp.bfloat16)

    code = lax.broadcasted_iota(jnp.int32, (32, LANES), 0).astype(jnp.float32)

    def one_hot(slots):
        return jnp.where(code == slots, 1.0, 0.0).astype(jnp.bfloat16)

    zero = jnp.zeros((32, LANES), jnp.bfloat16)
    for g in range(4):
        for c in range(8):
            cells = []
            for d in range(g * 32 + c, g * 32 + 32, 16):
                left = jnp.concatenate([one_hot(pairs[LANES + e : LANES + e + 1, :]) for e in (d, d + 8)], axis=1)
                q = [one_hot(pairs[e : e + 1, :]) for e in (d, d + 8)]
                right = jnp.concatenate(
                    [jnp.concatenate([q[0], zero], axis=1), jnp.concatenate([zero, q[1]], axis=1)], axis=0
                )
                cells.append(lax.dot_general(left, right, (((1,), (1,)), ((), ())), preferred_element_type=jnp.float32))
            cells = jnp.concatenate(cells, axis=1)
            for j in range(2):
                met[pl.ds(g * 256 + j * LANES + c, 16, stride=8), :] = cells[j * 16 : (j + 1) * 16]

    times = jnp.concatenate([met[g * 256 : (g + 1) * 256, :].astype(jnp.bfloat16) for g in range(4)], axis=1)
    summed = jnp.dot(times, final[...], preferred_element_type=jnp.float32)
    high = summed.astype(jnp.bfloat16)
    low = (summed - high.astype(jnp.float32)).astype(jnp.bfloat16)
    own = own_ref[...]
    part_ref[...] = lax.dot_general(
        jnp.concatenate([high[:, 0:256], low[:, 0:256]], axis=0),
        jnp.concatenate([own, own], axis=0),
        (((0,), (0,)), ((), ())),
        preferred_element_type=jnp.float32,
    )
    out_ref[0:256, :] = high[:, 256:512]
    out_ref[256:512, :] = low[:, 256:512]


def density_kernel(part_ref, summed_ref, other_ref, out_ref, full):
    other = other_ref[...]
    full[...] = part_ref[...] + lax.dot_general(
        summed_ref[...],
        jnp.concatenate([other, other], axis=0),
        (((0,), (0,)), ((), ())),
        preferred_element_type=jnp.float32,
    )
    lane = lane_index((8, LANES))
    upper = lax.broadcasted_iota(jnp.int32, (8, LANES), 0) < 4

    def tile(e, chunk):
        return full[e * 8 : (e + 1) * 8, chunk * LANES : (chunk + 1) * LANES]

    def put(t, value):
        out_ref[t * 8 : (t + 1) * 8, :] = value

    for e in range(FULL_TILES):
        for chunk in range(3):
            put(e * 3 + chunk, tile(e, chunk))
    for u in range(PACKED):
        two = jnp.where(lane < 64, tile(u, 3), pltpu.roll(tile(u + PACKED, 3), 64, 1))
        if u < 7:
            two = jnp.where((lane >= TAIL) & (lane < 64), pltpu.roll(tile(2 * PACKED, 3), TAIL - 8 * u, 1), two)
        put(FULL_TILES * 3 + u, two)
    for n in range(2):
        two = jnp.where(upper, tile(FULL_TILES, 2 * n), pltpu.roll(tile(FULL_TILES, 2 * n + 1), 4, 0))
        put(FULL_TILES * 3 + PACKED + n, two)


def sum_kernel(in_ref, out_ref):
    total = in_ref[0:24, :]
    for d in range(1, CHIPS // 2):
        total = total + in_ref[d * 24 : (d + 1) * 24, :]
    own = total[0:SLICE] + total[SLICE:24]
    twice = jnp.concatenate([own, own], axis=0)
    for d in range(CHIPS // 2):
        out_ref[d * 24 : (d + 1) * 24, :] = twice


def density_rows(first, second, start, stop):
    lane = lane_index((8, LANES))
    upper = lax.broadcasted_iota(jnp.int32, (8, LANES), 0) < 4
    packed = FULL_TILES * 3

    def tiles(half, e):
        def got(t):
            return half[t * 8 : (t + 1) * 8, :]

        if e == FULL_TILES:
            rest = [got(packed + PACKED), got(packed + PACKED + 1)]
            return [rest[0], pltpu.roll(rest[0], 4, 0), rest[1], pltpu.roll(rest[1], 4, 0)]
        if e < PACKED:
            strip = got(packed + e)
        elif e < 2 * PACKED:
            strip = pltpu.roll(got(packed + e - PACKED), 64, 1)
        else:
            strip = jnp.zeros((8, LANES), jnp.float32)
            for k in range(7):
                piece = pltpu.roll(got(packed + k), (8 * k - TAIL) % LANES, 1)
                strip = jnp.where((lane >= 8 * k) & (lane < 8 * k + 8), piece, strip)
        return [got(e * 3), got(e * 3 + 1), got(e * 3 + 2), strip]

    def turned(e):
        return [pltpu.roll(x, 4, 0) for x in tiles(second, e)]

    below = None
    for e in range(start, stop):
        if e < FULL_TILES:
            yield tiles(first, e)
            continue
        above = tiles(first, e) if e == FULL_TILES else turned(e - FULL_TILES - 1) if below is None else below
        below = turned(e - FULL_TILES)
        yield [jnp.where(upper, x, y) for x, y in zip(above, below)]


def put_rows(first, second, start, stop, chunk, out_hbm, out_ref, sent):
    copies = []
    for n, row in enumerate(density_rows(first, second, start, stop)):
        for c in range(3):
            out_ref[n * 8 : (n + 1) * 8, c * LANES : (c + 1) * LANES] = row[c]
        out_ref[n * 8 : (n + 1) * 8, 3 * LANES : 440] = row[3][:, 0:TAIL]
        if n % chunk == chunk - 1:
            here = slice((n - chunk + 1) * 8, (n + 1) * 8)
            there = slice((start + n - chunk + 1) * 8, (start + n + 1) * 8)
            copies.append(pltpu.make_async_copy(out_ref.at[here], out_hbm.at[there], sent.at[n // chunk]))
            copies[-1].start()
    for copy in copies:
        copy.wait()


def place_own_kernel(kept_ref, out_hbm, out_ref, sent):
    core = lax.axis_index("core")
    pl.when(core == 0)(lambda: put_rows(kept_ref, None, 0, FULL_TILES, 9, out_hbm, out_ref, sent))
    pl.when(core == 1)(lambda: put_rows(None, kept_ref, FULL_TILES + 1, 55, 9, out_hbm, out_ref, sent))


def place_other_kernel(kept_ref, given_ref, placed, out_hbm, out_ref, sent):
    del placed
    core = lax.axis_index("core")
    pl.when(core == 0)(lambda: put_rows(kept_ref, given_ref, FULL_TILES, 55, 7, out_hbm, out_ref, sent))
    pl.when(core == 1)(lambda: put_rows(given_ref, kept_ref, 0, FULL_TILES + 1, 7, out_hbm, out_ref, sent))


def exchange(x, axes, shape):
    return lax.all_to_all(x.reshape(shape), axes, 0, 0, tiled=True).reshape(x.shape)


def to_other_core(x):
    return lax.ppermute(x, "core", [(0, 1), (1, 0)])


def shards(final_amp, initial_amp, pair_final, pair_initial, map_final, map_initial, counts):
    vmem = pl.BlockSpec(memory_space=pltpu.VMEM)
    f32, bf16 = jnp.float32, jnp.bfloat16
    half = jax.ShapeDtypeStruct((CHIPS * SLICE, LANES), f32)

    def call(kernel, out_shape, n, scratch=(), cost=None):
        several = isinstance(out_shape, list)
        return pl.pallas_call(
            kernel,
            out_shape=out_shape,
            in_specs=[vmem] * n,
            out_specs=[vmem] * len(out_shape) if several else vmem,
            scratch_shapes=list(scratch),
            cost_estimate=cost,
            compiler_params=PARAMS,
        )

    messages = pl.pallas_call(
        send_kernel,
        out_shape=jax.ShapeDtypeStruct((DEVICES * MESSAGE, LANES), bf16),
        in_specs=[pl.BlockSpec(memory_space=pltpu.SMEM)] + [pl.BlockSpec(memory_space=pltpu.HBM)] * 6,
        out_specs=vmem,
        scratch_shapes=[
            pltpu.VMEM((6, 440, LANES), bf16),
            pltpu.VMEM((1, 1, LANES), jnp.int32),
            pltpu.VMEM((1, 1, LANES), jnp.int32),
            pltpu.VMEM((1, 4, 440), jnp.int32),
            pltpu.VMEM((1, 2, 440), jnp.int32),
            pltpu.VMEM((8, 512), jnp.int32),
            pltpu.VMEM((DEVICES * MESSAGE, LANES), f32),
            pltpu.SemaphoreType.DMA((6,)),
        ],
        compiler_params=PARAMS,
    )(
        counts,
        *(
            pltpu.with_memory_space_constraint(x, pltpu.HBM)
            for x in (
                jnp.swapaxes(final_amp, 2, 3),
                jnp.swapaxes(initial_amp, 2, 3),
                pair_final,
                pair_initial,
                map_final,
                map_initial,
            )
        )
    )
    received = exchange(messages, ALL, (DEVICES, MESSAGE, LANES))
    own = call(
        initial_kernel, jax.ShapeDtypeStruct((256, 512), bf16), 1, [pltpu.VMEM((DEVICES * 8, LANES), f32)]
    )(received)
    other = to_other_core(own)
    part, summed = call(
        times_kernel,
        [jax.ShapeDtypeStruct((256, 512), f32), jax.ShapeDtypeStruct((512, 256), bf16)],
        2,
        [
            pltpu.VMEM((DEVICES * MESSAGE, LANES), f32),
            pltpu.VMEM((2 * LANES, LANES), f32),
            pltpu.VMEM((512, 512), bf16),
            pltpu.VMEM((4 * 256, LANES), f32),
        ],
        pl.CostEstimate(flops=10**9, bytes_accessed=8 * 10**6, transcendentals=0),
    )(received, own)
    share = call(density_kernel, half, 3, [pltpu.VMEM((256, 512), f32)])(part, summed, other)
    shares = exchange(share, ACROSS_CHIPS, (CHIPS, 3, 4, LANES))
    copies = call(sum_kernel, half, 1)(shares)
    slices = exchange(copies, ACROSS_CHIPS, (CHIPS, 3, 4, LANES))
    hbm = pl.BlockSpec(memory_space=pltpu.HBM)
    other_slices = to_other_core(slices)
    density = jax.ShapeDtypeStruct((440, 440), f32)
    placed = pl.pallas_call(
        place_own_kernel,
        out_shape=density,
        in_specs=[vmem],
        out_specs=hbm,
        scratch_shapes=[pltpu.VMEM((FULL_TILES * 8, 440), f32), pltpu.SemaphoreType.DMA((3,))],
        cost_estimate=pl.CostEstimate(flops=10**6, bytes_accessed=4 * 10**6, transcendentals=0),
        compiler_params=PARAMS,
    )(slices)
    return pl.pallas_call(
        place_other_kernel,
        out_shape=density,
        in_specs=[vmem, vmem, hbm],
        out_specs=hbm,
        scratch_shapes=[pltpu.VMEM(((FULL_TILES + 1) * 8, 440), f32), pltpu.SemaphoreType.DMA((4,))],
        input_output_aliases={2: 0},
        compiler_params=PARAMS,
    )(slices, other_slices, placed)


def solution(mesh):
    cores = Mesh(mesh.devices.reshape(4, 2, 2, 2, 4), ALL)
    row, col = ("x", "y_hi", "core"), ("y_lo", "z")
    placed = (
        P(row, col, None, None),
        P(col, row, None, None),
        P(row, col, None),
        P(row, col, None),
        P(row, col, None),
        P(col, row, None),
        P(row, col),
    )
    return jax.shard_map(shards, mesh=cores, in_specs=placed, out_specs=P(), check_vma=False)
```

```python
import jax
import jax.numpy as jnp
from jax import lax
from jax.experimental import pallas as pl
from jax.experimental.pallas import tpu as pltpu
from jax.sharding import Mesh
from jax.sharding import PartitionSpec as P

LANES = 128
DEVICES = 128
CHIPS = 64
FINAL_ROWS = 16
MESSAGE = 24
SLICE = 12
HALF_ORB = 220
FULL_TILES = 27
PACKED = 13
TAIL = 56
DEAD = 64
ALL = ("x", "y_hi", "core", "y_lo", "z")
ACROSS_CHIPS = ("x", "y_hi", "y_lo", "z")
PARAMS = pltpu.CompilerParams(vmem_limit_bytes=48 * 1024 * 1024)


def lane_index(shape):
    return lax.broadcasted_iota(jnp.int32, shape, len(shape) - 1)


def send_kernel(counts, finals, initials, pairs_final, pairs_initial, maps_final, maps_initial, out_ref, *scratch):
    blocks, pf, pi, mf, mi, maps, wide, arrived = scratch
    pairs = [
        (finals.at[0], blocks.at[0:4]),
        (initials.at[0], blocks.at[4:6]),
        (maps_final, mf),
        (maps_initial, mi),
        (pairs_final, pf),
        (pairs_initial, pi),
    ]
    copies = [pltpu.make_async_copy(there, here, arrived.at[n]) for n, (there, here) in enumerate(pairs)]
    for copy in copies:
        copy.start()
    maps[...] = jnp.full(maps.shape, -1, jnp.int32)
    for copy in copies:
        copy.wait()
    maps[0:4, 0:HALF_ORB] = mf[0, :, 0:HALF_ORB]
    maps[0:4, 256 : 256 + HALF_ORB] = mf[0, :, HALF_ORB:440]
    maps[4:6, 0:440] = mi[0]
    slot = lane_index((1, LANES))
    q = pf[0]
    s = pi[0]
    q_code = jnp.where(slot < counts[0, 0], (q & 3) * 8 + (q >> 2), DEAD).astype(jnp.float32)
    s_code = ((s & 1) * 16 + (s >> 1)).astype(jnp.float32)
    q_code = jnp.broadcast_to(q_code, (8, LANES))
    s_code = jnp.broadcast_to(s_code, (8, LANES))
    info = [pltpu.roll(code, (96 - 32 * m) % LANES, 1) for code in (q_code, s_code) for m in range(4)]
    last = lane_index((8, LANES)) >= 96
    stored = lax.broadcasted_iota(jnp.int32, (440, 512), 0).astype(jnp.int16)
    one, zero = jnp.ones((440, 512), jnp.bfloat16), jnp.zeros((440, 512), jnp.bfloat16)
    for j in range(6):
        wanted = jnp.broadcast_to(maps[j : j + 1, :], (440, 512)).astype(jnp.int16)
        pick = jnp.where(stored == wanted, one, zero)
        ordered = lax.dot_general(blocks[j], pick, (((0,), (0,)), ((), ())), preferred_element_type=jnp.float32)
        for chunk in range(4):
            part = ordered[:, chunk * LANES : (chunk + 1) * LANES]
            if j >= 4:
                wide[pl.ds(j * 4 + chunk, DEVICES, stride=MESSAGE), :] = part
                continue
            core, place = chunk // 2, chunk % 2
            for group in range(16):
                other = core ^ (group % 2)
                rows = part[group * 8 : (group + 1) * 8]
                if place == 1:
                    rows = jnp.where(last, info[j * 2 + other], rows)
                first = (group // 2 * 2 + core) * 8 * MESSAGE + j * 4 + other * 2 + place
                wide[pl.ds(first, 8, stride=MESSAGE), :] = rows
    out_ref[...] = wide[...].astype(jnp.bfloat16)


def initial_kernel(in_ref, initial, wide):
    for d in range(0, DEVICES, 2):
        both = in_ref[d * MESSAGE : (d + 2) * MESSAGE, :].astype(jnp.float32)
        wide[d * 8 : (d + 1) * 8, :] = both[FINAL_ROWS:MESSAGE]
        wide[(d + 1) * 8 : (d + 2) * 8, :] = both[MESSAGE + FINAL_ROWS :]
    for j in range(2):
        for chunk in range(4):
            part = wide[pl.ds(j * 4 + chunk, DEVICES, stride=8), :].astype(jnp.bfloat16)
            initial[j * LANES : (j + 1) * LANES, chunk * LANES : (chunk + 1) * LANES] = part


def times_kernel(in_ref, own_ref, part_ref, out_ref, wide, pairs, final, met):
    wide[...] = in_ref[...].astype(jnp.float32)
    quarter = lane_index((LANES, LANES)) // 32
    for k in range(2):
        codes = jnp.zeros((LANES, LANES), jnp.float32)
        for m in range(4):
            piece = wide[pl.ds(1 + 2 * m + 8 * k, DEVICES, stride=MESSAGE), :]
            codes = jnp.where(quarter == m, pltpu.roll(piece, (32 * m - 96) % LANES, 1), codes)
        pairs[k * LANES : (k + 1) * LANES, :] = codes

    for r in range(16):
        for chunk in range(4):
            part = [wide[pl.ds(r * 8 * MESSAGE + j * 4 + chunk, 8, stride=MESSAGE), :] for j in range(4)]
            final[r * 32 : (r + 1) * 32, chunk * LANES : (chunk + 1) * LANES] = jnp.concatenate(part, axis=0).astype(jnp.bfloat16)

    code = lax.broadcasted_iota(jnp.int32, (32, LANES), 0).astype(jnp.float32)

    def one_hot(slots):
        return jnp.where(code == slots, 1.0, 0.0).astype(jnp.bfloat16)

    zero = jnp.zeros((32, LANES), jnp.bfloat16)
    for g in range(4):
        for c in range(8):
            cells = []
            for d in range(g * 32 + c, g * 32 + 32, 16):
                left = jnp.concatenate([one_hot(pairs[LANES + e : LANES + e + 1, :]) for e in (d, d + 8)], axis=1)
                q = [one_hot(pairs[e : e + 1, :]) for e in (d, d + 8)]
                right = jnp.concatenate(
                    [jnp.concatenate([q[0], zero], axis=1), jnp.concatenate([zero, q[1]], axis=1)], axis=0
                )
                cells.append(lax.dot_general(left, right, (((1,), (1,)), ((), ())), preferred_element_type=jnp.float32))
            cells = jnp.concatenate(cells, axis=1)
            for j in range(2):
                met[pl.ds(g * 256 + j * LANES + c, 16, stride=8), :] = cells[j * 16 : (j + 1) * 16]

    times = jnp.concatenate([met[g * 256 : (g + 1) * 256, :].astype(jnp.bfloat16) for g in range(4)], axis=1)
    summed = jnp.dot(times, final[...], preferred_element_type=jnp.float32)
    high = summed.astype(jnp.bfloat16)
    low = (summed - high.astype(jnp.float32)).astype(jnp.bfloat16)
    own = own_ref[...]
    part_ref[...] = lax.dot_general(
        jnp.concatenate([high[:, 0:256], low[:, 0:256]], axis=0),
        jnp.concatenate([own, own], axis=0),
        (((0,), (0,)), ((), ())),
        preferred_element_type=jnp.float32,
    )
    out_ref[0:256, :] = high[:, 256:512]
    out_ref[256:512, :] = low[:, 256:512]


def density_kernel(part_ref, summed_ref, other_ref, out_ref, full):
    other = other_ref[...]
    full[...] = part_ref[...] + lax.dot_general(
        summed_ref[...],
        jnp.concatenate([other, other], axis=0),
        (((0,), (0,)), ((), ())),
        preferred_element_type=jnp.float32,
    )
    lane = lane_index((8, LANES))
    upper = lax.broadcasted_iota(jnp.int32, (8, LANES), 0) < 4

    def tile(e, chunk):
        return full[e * 8 : (e + 1) * 8, chunk * LANES : (chunk + 1) * LANES]

    def put(t, value):
        out_ref[t * 8 : (t + 1) * 8, :] = value

    for e in range(FULL_TILES):
        for chunk in range(3):
            put(e * 3 + chunk, tile(e, chunk))
    for u in range(PACKED):
        two = jnp.where(lane < 64, tile(u, 3), pltpu.roll(tile(u + PACKED, 3), 64, 1))
        if u < 7:
            two = jnp.where((lane >= TAIL) & (lane < 64), pltpu.roll(tile(2 * PACKED, 3), TAIL - 8 * u, 1), two)
        put(FULL_TILES * 3 + u, two)
    for n in range(2):
        two = jnp.where(upper, tile(FULL_TILES, 2 * n), pltpu.roll(tile(FULL_TILES, 2 * n + 1), 4, 0))
        put(FULL_TILES * 3 + PACKED + n, two)


def sum_kernel(in_ref, out_ref):
    total = in_ref[0:24, :]
    for d in range(1, CHIPS // 2):
        total = total + in_ref[d * 24 : (d + 1) * 24, :]
    own = total[0:SLICE] + total[SLICE:24]
    twice = jnp.concatenate([own, own], axis=0)
    for d in range(CHIPS // 2):
        out_ref[d * 24 : (d + 1) * 24, :] = twice


def density_rows(first, second, start, stop):
    lane = lane_index((8, LANES))
    upper = lax.broadcasted_iota(jnp.int32, (8, LANES), 0) < 4
    packed = FULL_TILES * 3

    def tiles(half, e):
        def got(t):
            return half[t * 8 : (t + 1) * 8, :]

        if e == FULL_TILES:
            rest = [got(packed + PACKED), got(packed + PACKED + 1)]
            return [rest[0], pltpu.roll(rest[0], 4, 0), rest[1], pltpu.roll(rest[1], 4, 0)]
        if e < PACKED:
            strip = got(packed + e)
        elif e < 2 * PACKED:
            strip = pltpu.roll(got(packed + e - PACKED), 64, 1)
        else:
            strip = jnp.zeros((8, LANES), jnp.float32)
            for k in range(7):
                piece = pltpu.roll(got(packed + k), (8 * k - TAIL) % LANES, 1)
                strip = jnp.where((lane >= 8 * k) & (lane < 8 * k + 8), piece, strip)
        return [got(e * 3), got(e * 3 + 1), got(e * 3 + 2), strip]

    def turned(e):
        return [pltpu.roll(x, 4, 0) for x in tiles(second, e)]

    below = None
    for e in range(start, stop):
        if e < FULL_TILES:
            yield tiles(first, e)
            continue
        above = tiles(first, e) if e == FULL_TILES else turned(e - FULL_TILES - 1) if below is None else below
        below = turned(e - FULL_TILES)
        yield [jnp.where(upper, x, y) for x, y in zip(above, below)]


def put_rows(first, second, start, stop, chunk, out_hbm, out_ref, sent):
    copies = []
    for n, row in enumerate(density_rows(first, second, start, stop)):
        for c in range(3):
            out_ref[n * 8 : (n + 1) * 8, c * LANES : (c + 1) * LANES] = row[c]
        out_ref[n * 8 : (n + 1) * 8, 3 * LANES : 440] = row[3][:, 0:TAIL]
        if n % chunk == chunk - 1:
            here = slice((n - chunk + 1) * 8, (n + 1) * 8)
            there = slice((start + n - chunk + 1) * 8, (start + n + 1) * 8)
            copies.append(pltpu.make_async_copy(out_ref.at[here], out_hbm.at[there], sent.at[n // chunk]))
            copies[-1].start()
    for copy in copies:
        copy.wait()


def place_own_kernel(kept_ref, out_hbm, out_ref, sent):
    core = lax.axis_index("core")
    pl.when(core == 0)(lambda: put_rows(kept_ref, None, 0, FULL_TILES, 9, out_hbm, out_ref, sent))
    pl.when(core == 1)(lambda: put_rows(None, kept_ref, FULL_TILES + 1, 55, 9, out_hbm, out_ref, sent))


def place_other_kernel(kept_ref, given_ref, placed, out_hbm, out_ref, sent):
    del placed
    core = lax.axis_index("core")
    pl.when(core == 0)(lambda: put_rows(kept_ref, given_ref, FULL_TILES, 55, 2, out_hbm, out_ref, sent))
    pl.when(core == 1)(lambda: put_rows(given_ref, kept_ref, 0, FULL_TILES + 1, 2, out_hbm, out_ref, sent))


def exchange(x, axes, shape):
    return lax.all_to_all(x.reshape(shape), axes, 0, 0, tiled=True).reshape(x.shape)


def to_other_core(x):
    return lax.ppermute(x, "core", [(0, 1), (1, 0)])


def shards(final_amp, initial_amp, pair_final, pair_initial, map_final, map_initial, counts):
    vmem = pl.BlockSpec(memory_space=pltpu.VMEM)
    f32, bf16 = jnp.float32, jnp.bfloat16
    half = jax.ShapeDtypeStruct((CHIPS * SLICE, LANES), f32)

    def call(kernel, out_shape, n, scratch=(), cost=None):
        several = isinstance(out_shape, list)
        return pl.pallas_call(
            kernel,
            out_shape=out_shape,
            in_specs=[vmem] * n,
            out_specs=[vmem] * len(out_shape) if several else vmem,
            scratch_shapes=list(scratch),
            cost_estimate=cost,
            compiler_params=PARAMS,
        )

    messages = pl.pallas_call(
        send_kernel,
        out_shape=jax.ShapeDtypeStruct((DEVICES * MESSAGE, LANES), bf16),
        in_specs=[pl.BlockSpec(memory_space=pltpu.SMEM)] + [pl.BlockSpec(memory_space=pltpu.HBM)] * 6,
        out_specs=vmem,
        scratch_shapes=[
            pltpu.VMEM((6, 440, LANES), bf16),
            pltpu.VMEM((1, 1, LANES), jnp.int32),
            pltpu.VMEM((1, 1, LANES), jnp.int32),
            pltpu.VMEM((1, 4, 440), jnp.int32),
            pltpu.VMEM((1, 2, 440), jnp.int32),
            pltpu.VMEM((8, 512), jnp.int32),
            pltpu.VMEM((DEVICES * MESSAGE, LANES), f32),
            pltpu.SemaphoreType.DMA((6,)),
        ],
        compiler_params=PARAMS,
    )(
        counts,
        *(
            pltpu.with_memory_space_constraint(x, pltpu.HBM)
            for x in (
                jnp.swapaxes(final_amp, 2, 3),
                jnp.swapaxes(initial_amp, 2, 3),
                pair_final,
                pair_initial,
                map_final,
                map_initial,
            )
        )
    )
    received = exchange(messages, ALL, (DEVICES, MESSAGE, LANES))
    own = call(
        initial_kernel, jax.ShapeDtypeStruct((256, 512), bf16), 1, [pltpu.VMEM((DEVICES * 8, LANES), f32)]
    )(received)
    other = to_other_core(own)
    part, summed = call(
        times_kernel,
        [jax.ShapeDtypeStruct((256, 512), f32), jax.ShapeDtypeStruct((512, 256), bf16)],
        2,
        [
            pltpu.VMEM((DEVICES * MESSAGE, LANES), f32),
            pltpu.VMEM((2 * LANES, LANES), f32),
            pltpu.VMEM((512, 512), bf16),
            pltpu.VMEM((4 * 256, LANES), f32),
        ],
        pl.CostEstimate(flops=10**9, bytes_accessed=8 * 10**6, transcendentals=0),
    )(received, own)
    share = call(density_kernel, half, 3, [pltpu.VMEM((256, 512), f32)])(part, summed, other)
    shares = exchange(share, ACROSS_CHIPS, (CHIPS, 3, 4, LANES))
    copies = call(sum_kernel, half, 1)(shares)
    slices = exchange(copies, ACROSS_CHIPS, (CHIPS, 3, 4, LANES))
    hbm = pl.BlockSpec(memory_space=pltpu.HBM)
    other_slices = to_other_core(slices)
    density = jax.ShapeDtypeStruct((440, 440), f32)
    placed = pl.pallas_call(
        place_own_kernel,
        out_shape=density,
        in_specs=[vmem],
        out_specs=hbm,
        scratch_shapes=[pltpu.VMEM((FULL_TILES * 8, 440), f32), pltpu.SemaphoreType.DMA((3,))],
        cost_estimate=pl.CostEstimate(flops=10**6, bytes_accessed=4 * 10**6, transcendentals=0),
        compiler_params=PARAMS,
    )(slices)
    return pl.pallas_call(
        place_other_kernel,
        out_shape=density,
        in_specs=[vmem, vmem, hbm],
        out_specs=hbm,
        scratch_shapes=[pltpu.VMEM(((FULL_TILES + 1) * 8, 440), f32), pltpu.SemaphoreType.DMA((14,))],
        input_output_aliases={2: 0},
        compiler_params=PARAMS,
    )(slices, other_slices, placed)


def solution(mesh):
    cores = Mesh(mesh.devices.reshape(4, 2, 2, 2, 4), ALL)
    row, col = ("x", "y_hi", "core"), ("y_lo", "z")
    placed = (
        P(row, col, None, None),
        P(col, row, None, None),
        P(row, col, None),
        P(row, col, None),
        P(row, col, None),
        P(col, row, None),
        P(row, col),
    )
    return jax.shard_map(shards, mesh=cores, in_specs=placed, out_specs=P(), check_vma=False)
```
